256 devices in a mesh: ctx: 16 (over y, x_lo, core), head: 16 (over x_hi, z).
Axes of the slice: x: 4 (x_hi: 2, x_lo: 2; x = x_hi * 2 + x_lo), y: 4, z: 8, core: 2. Of those that a mesh axis runs over, the one named last changes fastest.
Arguments:
- queries: bfloat16 [5120, 4096], P('ctx', 'head'), may hold values from -15 to 15
- keys: bfloat16 [5120, 4096], P('ctx', 'head'), may hold values from -15 to 15
- values: bfloat16 [5120, 4096], P('ctx', 'head'), may hold values from -6 to 6
- out_grad: bfloat16 [5120, 4096], P('ctx', 'head'), may hold values from -6 to 6
- out_weight: bfloat16 [4096, 4096], P('head'), may hold values from -0.09375 to 0.09375
- doc_lengths: int32 [8], replicated, may hold values from 1 to 3840, 5120 in all
- loss_numer: int32 [5120], P('ctx'), may hold values from 0 to 8
Outputs:
- grad_queries: bfloat16 [5120, 4096], P('ctx', 'head')
- grad_keys: bfloat16 [5120, 4096], P('ctx', 'head')
- grad_values: bfloat16 [5120, 4096], P('ctx', 'head')
- grad_out_weight: float32 [4096, 4096], P('head', 'ctx')
The draws below stay inside these ranges and needn't reach their ends.
Inputs may be any that keep to these rules, and one draw needn't show every extreme that they name: `doc_lengths`: 8 positive lengths that sum to 5120; the longest is exactly three quarters of 5120, rounded down.
All inputs are finite; a program needn't handle non-finite values.
Results may differ from the reference program's by a relative error of at most 0.035.
Values may be sent and summed in bfloat16 or wider, within the bound.
No kernel may reach another device: no remote copies, remote signals or barrier semaphores. Data moves between devices by JAX's collectives and lax.ppermute only.
A program may use at most 64 MiB of HBM per device.

```python
import math
import jax
import jax.numpy as jnp
import numpy as np
from jax import lax

D = 4096
HD = 128
DOCS = 8
HEADS = 32
TOKENS = 5120


def draw_queries(key, part):
    key = jax.random.fold_in(key, 11)
    field = 1.6 * jnp.clip(jax.random.normal(key, (TOKENS, HEADS * HD), jnp.float32), -4.0, 4.0)
    return field.astype(jnp.bfloat16)


def draw_keys(key, part):
    key = jax.random.fold_in(key, 12)
    field = 1.6 * jnp.clip(jax.random.normal(key, (TOKENS, HEADS * HD), jnp.float32), -4.0, 4.0)
    return field.astype(jnp.bfloat16)


def place_ends(values, own_key, least, high):
    dims = values.shape
    spot = [jax.random.randint(jax.random.fold_in(own_key, axis), (), 0, dims[axis]) for axis in range(len(dims))]
    values = values.at[tuple(spot)].set(least)
    longest = dims.index(max(dims))
    spot[longest] = (spot[longest] + 1) % dims[longest]
    return values.at[tuple(spot)].set(high)


def steps_of(stream_key, extent, split, low, top_value):
    gain, own = 1.0, jax.random.fold_in(stream_key, 6)
    for position, blocks in split:
        draws = jnp.exp(jax.random.uniform(jax.random.fold_in(own, position), (blocks,), jnp.float32, low / len(split), top_value / len(split)))
        gain = gain * jnp.repeat(draws, extent[position] // blocks).reshape([-1 if axis == position else 1 for axis in range(len(extent))])
    return gain


def profile(number_of, total, most, lean):
    weights = [(1 << 20) // math.isqrt(grade ** lean) + 1 for grade in range(2, number_of + 1)]
    spare, given = total - most - (number_of - 1), [1] * (number_of - 1)
    while spare > 0:
        free = [i for i in range(number_of - 1) if given[i] < most]
        pool, left = sum([weights[i] for i in free]), spare
        for i in free:
            addition = min(most - given[i], max(1, left * weights[i] // pool), spare)
            given[i] = given[i] + addition
            spare = spare - addition
    return np.array([most] + given)


def ragged_sizes(key, count, total, reach, lean):
    if count == 2:
        one = jax.random.randint(key, (), max(1, total - reach), min(reach, total - 1) + 1)
        return jnp.stack([one, total - one])
    sizes = jnp.asarray(profile(count, total, reach, lean), jnp.int32)
    pairs = (count - 1) // 2
    source_of, taker = sizes[1:1 + 2 * pairs:2], sizes[2:2 + 2 * pairs:2]
    room = jnp.minimum(source_of - 1, reach - taker)
    shifted = jax.random.randint(jax.random.fold_in(key, 1), (pairs,), 0, 1 << 20) % (room + 1)
    sizes = sizes.at[1:1 + 2 * pairs:2].set(source_of - shifted).at[2:2 + 2 * pairs:2].set(taker + shifted)
    return sizes[jax.random.permutation(jax.random.fold_in(key, 2), count)]


def scatter_about(key, extent, deviation, most, pieces=(), kind=jnp.bfloat16):
    values = jax.random.normal(key, extent, jnp.float32) * deviation
    if len(pieces) > 0:
        values = steps_of(key, extent, pieces, -0.22, 0.18) * values
    return jnp.clip(values, min=-most, max=most).astype(kind)


def setup_inputs(seed: int = 0) -> dict:
    splits = jax.random.split(jax.random.key(seed), 8)
    queries = draw_queries(jax.random.fold_in(splits[7], 71), 0)
    keys = draw_keys(jax.random.fold_in(splits[7], 71), 0)
    values = scatter_about(splits[2], (TOKENS, HEADS * HD), 1.0, 6.0, ((0, 16), (1, 16)))
    out_grad = scatter_about(splits[3], (TOKENS, D), 1.0, 6.0, ((0, 16), (1, 16)))
    out_weight = scatter_about(splits[4], (HEADS * HD, D), (HEADS * HD) ** -0.5, 0.09375, ((0, 16),))
    doc_lengths = ragged_sizes(splits[5], DOCS, TOKENS, 3 * TOKENS // 4, 2).astype(jnp.int32)
    loss_numer = place_ends(jax.random.randint(splits[6], (TOKENS,), 0, 9), jax.random.fold_in(splits[6], 1), 0, 8).astype(jnp.int32)
    return {"queries": queries, "keys": keys, "values": values, "out_grad": out_grad, "out_weight": out_weight, "doc_lengths": doc_lengths, "loss_numer": loss_numer}


def reference(queries, keys, values, out_grad, out_weight, doc_lengths, loss_numer):
    factor = HD ** -0.5
    doc_ends = jnp.cumsum(doc_lengths).astype(jnp.int32)
    positions = jnp.arange(TOKENS, dtype=jnp.int32)
    doc_index = jnp.sum((positions[:, None] >= doc_ends[None, :]).astype(jnp.int32), axis=1)
    same_doc = doc_index[:, None] == doc_index[None, :]

    def by_head(array):
        return array.reshape(TOKENS, HEADS, HD).transpose(1, 0, 2)

    def unhead(array):
        return array.transpose(1, 0, 2).reshape(TOKENS, HEADS * HD)

    def scores_of(query, key):
        return jnp.dot(query, key.T, preferred_element_type=jnp.float32) * factor

    def forward(inputs):
        query, key, value = inputs
        scores = scores_of(query, key)
        row_max = jnp.max(jnp.where(same_doc, scores, -jnp.inf), axis=1)
        weights = jnp.where(same_doc, jnp.exp(scores - row_max[:, None]), 0.0)
        row_sum = jnp.sum(weights, axis=1)
        output = jnp.dot(weights.astype(jnp.bfloat16), value, preferred_element_type=jnp.float32) / row_sum[:, None]
        return output.astype(jnp.bfloat16), row_max + jnp.log(row_sum)

    head_out, log_total = lax.map(forward, (by_head(queries), by_head(keys), by_head(values)))
    attended = unhead(head_out)
    scaled = (out_grad.astype(jnp.float32) * (loss_numer.astype(jnp.float32) / 8.0)[:, None]).astype(jnp.bfloat16)
    dout = jnp.dot(scaled, out_weight.T, preferred_element_type=jnp.float32).astype(jnp.bfloat16)
    grad_out_weight = jnp.dot(attended.T, scaled, preferred_element_type=jnp.float32)

    def backward(inputs):
        query, key, value, dout_head, output, total = inputs
        scores = scores_of(query, key)
        prob = jnp.where(same_doc, jnp.exp(scores - total[:, None]), 0.0)
        grad_value = jnp.dot(prob.astype(jnp.bfloat16).T, dout_head, preferred_element_type=jnp.float32)
        grad_prob = jnp.dot(dout_head, value.T, preferred_element_type=jnp.float32)
        row_dot = jnp.sum(dout_head.astype(jnp.float32) * output.astype(jnp.float32), axis=1)
        grad_score = (prob * (grad_prob - row_dot[:, None])).astype(jnp.bfloat16)
        grad_query = jnp.dot(grad_score, key, preferred_element_type=jnp.float32) * factor
        grad_key = jnp.dot(grad_score.T, query, preferred_element_type=jnp.float32) * factor
        return grad_query.astype(jnp.bfloat16), grad_key.astype(jnp.bfloat16), grad_value.astype(jnp.bfloat16)

    grad_q, grad_k, grad_v = lax.map(backward, (by_head(queries), by_head(keys), by_head(values), by_head(dout), head_out, log_total))
    return unhead(grad_q), unhead(grad_k), unhead(grad_v), grad_out_weight
```

```python
import math

import jax
import jax.numpy as jnp
from jax import lax
from jax.experimental import pallas as pl
from jax.experimental.pallas import tpu as pltpu
from jax.sharding import Mesh, PartitionSpec as P

ROWS = 320
PAIR = 640
HD = 128
NQ = 1280
COLS = 256
FACTOR = HD ** -0.5
SCALE2 = FACTOR * math.log2(math.e)
FLOOR = -1e30
MASKED = -2e30
NY = 4
NZ = 8
VMEM_LIMIT = 48 * 1024 * 1024

F32 = jnp.float32
BF16 = jnp.bfloat16

NT = (((1,), (1,)), ((), ()))
NN = (((1,), (0,)), ((), ()))
TN = (((0,), (0,)), ((), ()))


def dot(a, b, dims):
    return lax.dot_general(a, b, dims, preferred_element_type=F32)


CORE, QBASE, KBASE, ENDS = 0, 1, 3, 7


def doc_of(pos, info):
    total = jnp.zeros_like(pos)
    for i in range(8):
        total = total + jnp.where(pos >= info[ENDS + i], 1, 0)
    return total


def token_of(base, row, info):
    turned = row + info[CORE] * ROWS
    return base + jnp.where(turned >= PAIR, turned - PAIR, turned)


def query_docs(half, info):
    row = lax.broadcasted_iota(jnp.int32, (1, PAIR), 1)
    return doc_of(token_of(info[QBASE + half], row, info), info)


def key_docs(block, start, size, info):
    row = lax.broadcasted_iota(jnp.int32, (size, 1), 0) + start
    return doc_of(token_of(info[KBASE + block], row, info), info)


def relation(half, block, info):
    qb, kb = info[QBASE + half], info[KBASE + block]
    q_low, q_high = doc_of(qb, info), doc_of(qb + PAIR - 1, info)
    k_low, k_high = doc_of(kb, info), doc_of(kb + PAIR - 1, info)
    meets = (q_high >= k_low) & (k_high >= q_low)
    whole = (q_low == q_high) & (k_low == k_high) & (q_low == k_low)
    return meets, whole


FWD_CHUNK = 320


def forward_kernel(info, q_own, q_far, kv0, kv1, kv2, kv3, out_ref, lse_ref, acc, m_ref, l_ref):
    kvs = (kv0, kv1, kv2, kv3)
    for half, q_ref in enumerate((q_own, q_far)):
        acc[...] = jnp.zeros_like(acc)
        m_ref[...] = jnp.full_like(m_ref, FLOOR)
        l_ref[...] = jnp.zeros_like(l_ref)
        for block in range(NY):
            kv_ref = kvs[block]
            meets, whole = relation(half, block, info)

            def run(masked, kv_ref=kv_ref, block=block, half=half, q_ref=q_ref):
                def step(i, _):
                    start = pl.multiple_of(i * FWD_CHUNK, FWD_CHUNK)
                    keys = kv_ref[pl.ds(start, FWD_CHUNK), :HD]
                    vals = kv_ref[pl.ds(start, FWD_CHUNK), HD:]
                    s = dot(keys, q_ref[...], NT) * SCALE2
                    if masked:
                        same = key_docs(block, start, FWD_CHUNK, info) == query_docs(half, info)
                        s = jnp.where(same, s, MASKED)
                    old = m_ref[...]
                    new = jnp.maximum(old, jnp.max(s, axis=0, keepdims=True))
                    p = jnp.exp2(s - new)
                    shrink = jnp.exp2(old - new)
                    m_ref[...] = new
                    l_ref[...] = l_ref[...] * shrink + jnp.sum(p, axis=0, keepdims=True)
                    acc[...] = acc[...] * shrink + dot(vals, p.astype(BF16), TN)
                    return 0

                lax.fori_loop(0, PAIR // FWD_CHUNK, step, 0)

            @pl.when(meets & whole)
            def _():
                run(False)

            @pl.when(meets & jnp.logical_not(whole))
            def _():
                run(True)

        total = l_ref[...]
        seen = total > 0
        safe = jnp.where(seen, total, 1.0)
        columns = pl.ds(half * PAIR, PAIR)
        out_ref[:, columns] = (acc[...] / safe).astype(BF16)
        lse_ref[:, columns] = jnp.where(seen, m_ref[...] + jnp.log2(safe), FLOOR)


def merge_kernel(mine, mine_lse, theirs, theirs_lse, att_ref, lse_ref, keep_ref, give_ref):
    for half in range(2):
        here, there = pl.ds(half * PAIR, PAIR), pl.ds((1 - half) * PAIR, PAIR)
        a, b = mine_lse[:, here], theirs_lse[:, there]
        top = jnp.maximum(a, b)
        lse = top + jnp.log2(jnp.exp2(a - top) + jnp.exp2(b - top))
        lse_ref[:, here] = lse
        att = mine[:, here].astype(F32) * jnp.exp2(a - lse) + theirs[:, there].astype(F32) * jnp.exp2(b - lse)
        att_ref[:, here] = att.astype(BF16)
        if half == 0:
            rows = att.T.astype(BF16)
            keep_ref[...] = rows[:ROWS]
            give_ref[...] = rows[ROWS:]


def piece_list(refs):
    out = []
    for chain in range(2):
        own = refs[chain * 9 : chain * 9 + 9]
        for ref, distance in zip(own[:7], (0, 1, -1, 2, -2, 3, -3)):
            out.append((ref, chain, distance, 0, ROWS))
        out.append((own[7], chain, 4, 0, ROWS // 2))
        out.append((own[8], chain, 4, ROWS // 2, ROWS // 2))
    return out


def group_of(place, chain, distance):
    x_hi = place[1] if chain == 0 else 1 - place[1]
    z = lax.rem(place[2] - distance + NZ, NZ)
    return x_hi, z


def dout_kernel(place, w_ref, *refs):
    pieces, (keep_ref, give_ref, acc) = refs[:18], refs[18:]
    acc[...] = jnp.zeros_like(acc)
    for ref, chain, distance, first, count in piece_list(pieces):
        x_hi, z = group_of(place, chain, distance)
        columns = pl.ds(pl.multiple_of((x_hi * NZ + z) * COLS, COLS), COLS)
        acc[first : first + count, :] += dot(ref[...], w_ref[:, columns], NT)
    core = place[0]
    keep = pl.ds(pl.multiple_of(core * HD, HD), HD)
    give = pl.ds(pl.multiple_of((1 - core) * HD, HD), HD)
    keep_ref[...] = acc[:, keep].astype(BF16)
    give_ref[...] = acc[:, give].astype(BF16)


def weight_kernel(place, att_own, att_other, *refs):
    pieces, (keep_ref, give_ref, both, whole) = refs[:18], refs[18:]
    core = place[0]
    both[:, pl.ds(pl.multiple_of(core * HD, HD), HD)] = att_own[...]
    both[:, pl.ds(pl.multiple_of((1 - core) * HD, HD), HD)] = att_other[...]
    listed = piece_list(pieces)
    for chain in range(2):
        own = listed[chain * 9 : chain * 9 + 9]
        for ref, _, distance, first, count in own:
            if distance == 4:
                whole[first : first + count, :] = ref[...]
                if first == 0:
                    continue
                ref = whole
            x_hi, z = group_of(place, chain, distance)
            y_to, lo_to, core_to = x_hi * 2 + z // 4, lax.rem(z // 2, 2), lax.rem(z, 2)
            slot = lax.rem(y_to - place[3] + NY, NY) * 2 + jnp.where(lo_to == place[4], 0, 1)
            term = dot(both[...], ref[...], TN).astype(BF16)

            @pl.when(core_to == core)
            def _(term=term, slot=slot):
                keep_ref[slot] = term

            @pl.when(core_to != core)
            def _(term=term, slot=slot):
                give_ref[slot] = term


BWD_CHUNK = 320


def backward_kernel(block, first, info, *refs):
    q_own, q_far, do0, do1, do2, do3, lse_ref, att_ref, kv_ref = refs[:9]
    if first:
        gq_ref, gkv_ref, grad_out, row_dot, gk_acc, gv_acc = refs[9:]
        gq_in = None
    else:
        gq_in, gq_ref, gkv_ref, grad_out, row_dot, gk_acc, gv_acc = refs[9:]
    for i, ref in enumerate((do0, do1, do2, do3)):
        grad_out[i * ROWS : (i + 1) * ROWS, :] = ref[...]
    for half in range(2):
        here = pl.ds(half * PAIR, PAIR)
        turned = grad_out[here, :].astype(F32).T
        row_dot[:, here] = jnp.sum(turned * att_ref[:, here].astype(F32), axis=0, keepdims=True)
    if first:
        gq_ref[...] = jnp.zeros_like(gq_ref)
    else:
        gq_ref[...] = gq_in[...]
    gk_acc[...] = jnp.zeros_like(gk_acc)
    gv_acc[...] = jnp.zeros_like(gv_acc)
    for half, q_ref in enumerate((q_own, q_far)):
        meets, whole = relation(half, block, info)
        here = pl.ds(half * PAIR, PAIR)

        def run(masked, half=half, q_ref=q_ref, here=here):
            def step(i, _):
                start = pl.multiple_of(i * BWD_CHUNK, BWD_CHUNK)
                rows = pl.ds(start, BWD_CHUNK)
                keys = kv_ref[rows, :HD]
                vals = kv_ref[rows, HD:]
                queries = q_ref[...]
                grads = grad_out[here, :]
                s = dot(keys, queries, NT) * SCALE2 - lse_ref[:, here]
                if masked:
                    same = key_docs(block, start, BWD_CHUNK, info) == query_docs(half, info)
                    s = jnp.where(same, s, MASKED)
                p = jnp.exp2(s)
                gv_acc[rows, :] += dot(p.astype(BF16), grads, NN)
                gp = dot(vals, grads, NT)
                gs = (p * (gp - row_dot[:, here])).astype(BF16)
                gk_acc[rows, :] += dot(gs, queries, NN)
                gq_ref[:, here] += dot(keys, gs, TN)
                return 0

            lax.fori_loop(0, PAIR // BWD_CHUNK, step, 0)

        @pl.when(meets & whole)
        def _():
            run(False)

        @pl.when(meets & jnp.logical_not(whole))
        def _():
            run(True)

    gkv_ref[:, :HD] = (gk_acc[...] * FACTOR).astype(gkv_ref.dtype)
    gkv_ref[:, HD:] = gv_acc[...].astype(gkv_ref.dtype)


SMEM = pl.BlockSpec(memory_space=pltpu.SMEM)
VMEM = pl.BlockSpec(memory_space=pltpu.VMEM)


def call(kernel, name, scalars, arrays, outs, scratch, flops, aliases=None):
    moved = sum(a.size * a.dtype.itemsize for a in arrays) + sum(math.prod(s) * jnp.dtype(t).itemsize for s, t in outs)
    return pl.pallas_call(
        kernel,
        name=name,
        out_shape=[jax.ShapeDtypeStruct(s, t) for s, t in outs],
        in_specs=[SMEM] + [VMEM] * len(arrays),
        out_specs=[VMEM] * len(outs),
        scratch_shapes=[pltpu.VMEM(s, t) for s, t in scratch],
        input_output_aliases=aliases or {},
        cost_estimate=pl.CostEstimate(flops=int(flops), bytes_accessed=int(moved), transcendentals=0),
        compiler_params=pltpu.CompilerParams(vmem_limit_bytes=VMEM_LIMIT),
    )(scalars, *arrays)


def shift(x, axis, step):
    size = {"y": NY, "x_lo": 2, "core": 2, "x_hi": 2, "z": NZ}[axis]
    return lax.ppermute(x, axis, [(i, (i + step) % size) for i in range(size)])


def swap_both(x):
    return lax.ppermute(x, ("x_lo", "core"), [(i, 3 - i) for i in range(4)])


def half_columns(x, which):
    return lax.dynamic_slice_in_dim(x, which * HD, HD, 1)


def on_device(queries, keys, values, out_grad, out_weight, doc_lengths, loss_numer):
    y, x_lo, core = lax.axis_index("y"), lax.axis_index("x_lo"), lax.axis_index("core")
    x_hi, z = lax.axis_index("x_hi"), lax.axis_index("z")
    other = 1 - core
    place = jnp.stack([core, x_hi, z, y, x_lo]).astype(jnp.int32)
    block_y = [y, (y + 3) % NY, (y + 1) % NY, (y + 2) % NY]
    info = jnp.concatenate(
        [
            jnp.stack(
                [core, y * NQ + x_lo * PAIR, y * NQ + (1 - x_lo) * PAIR] + [b * NQ + x_lo * PAIR for b in block_y]
            ).astype(jnp.int32),
            jnp.cumsum(doc_lengths),
        ]
    )

    scaled = (out_grad.astype(F32) * (loss_numer.astype(F32) / 8.0)[:, None]).astype(BF16)

    chains = []
    for first in (scaled, shift(scaled, "x_hi", 1)):
        up, down = [first], [first]
        for _ in range(3):
            up.append(shift(up[-1], "z", 1))
            down.append(shift(down[-1], "z", -1))
        far_up = shift(up[3][: ROWS // 2], "z", 1)
        far_down = shift(down[3][ROWS // 2 :], "z", -1)
        chains += [first, up[1], down[1], up[2], down[2], up[3], down[3], far_up, far_down]

    sent = shift(jnp.concatenate([half_columns(a, other) for a in (keys, values, queries)], axis=1), "core", 1)
    held = jnp.concatenate([half_columns(a, core) for a in (keys, values, queries)], axis=1)
    both = jnp.concatenate([held, sent], axis=0)
    kv, q_own = both[:, : 2 * HD], both[:, 2 * HD :]
    kvs = [kv, shift(kv, "y", 1), shift(kv, "y", -1), shift(kv, "y", 2)]
    q_far = shift(q_own, "x_lo", 1)

    out_part, lse_part = call(
        forward_kernel,
        "forward",
        info,
        [q_own, q_far] + kvs,
        [((HD, NQ), BF16), ((1, NQ), F32)],
        [((HD, PAIR), F32), ((1, PAIR), F32), ((1, PAIR), F32)],
        2 * 2 * NQ * 2 * NQ * HD * 2,
    )
    att, lse, att_keep, att_give = call(
        lambda info, *refs: merge_kernel(*refs),
        "merge",
        info,
        [out_part, lse_part, shift(out_part, "x_lo", 1), shift(lse_part, "x_lo", 1)],
        [((HD, NQ), BF16), ((1, NQ), F32), ((ROWS, HD), BF16), ((ROWS, HD), BF16)],
        [],
        1e6,
    )
    att_other = shift(att_give, "core", 1)

    do_keep, do_give = call(
        dout_kernel,
        "dout",
        place,
        [out_weight] + chains,
        [((ROWS, HD), BF16), ((ROWS, HD), BF16)],
        [((ROWS, COLS), F32)],
        2 * ROWS * 4096 * COLS,
    )
    dos = [do_keep, shift(do_give, "core", 1), shift(do_keep, "x_lo", 1), swap_both(do_give)]

    gw_keep, gw_give = call(
        weight_kernel,
        "weight",
        place,
        [att_keep, att_other] + chains,
        [((8, COLS, COLS), BF16), ((8, COLS, COLS), BF16)],
        [((ROWS, COLS), BF16), ((ROWS, COLS), BF16)],
        2 * ROWS * 4096 * COLS,
    )
    gw = gw_keep.astype(F32) + shift(gw_give, "core", 1).astype(F32)
    gw_sum = gw[0:2]
    for step in (1, 2, 3):
        gw_sum = gw_sum + shift(gw[2 * step : 2 * step + 2].astype(BF16), "y", step).astype(F32)
    grad_out_weight = gw_sum[0] + shift(gw_sum[1].astype(BF16), "x_lo", 1).astype(F32)

    gq = None
    key_parts = {}
    for block in (3, 1, 2, 0):
        first = gq is None
        arrays = [q_own, q_far] + dos + [lse, att, kvs[block]] + ([] if first else [gq])
        gq, key_parts[block] = call(
            lambda *refs, block=block, first=first: backward_kernel(block, first, *refs),
            "backward",
            info,
            arrays,
            [((HD, NQ), F32), ((PAIR, 2 * HD), F32 if block == 0 else BF16)],
            [((NQ, HD), BF16), ((1, NQ), F32), ((PAIR, HD), F32), ((PAIR, HD), F32)],
            2 * 5 * NQ * PAIR * HD * 2,
            None if first else {len(arrays): 0},
        )
    gkv = key_parts[0]
    for block, step in ((3, 2), (1, -1), (2, 1)):
        gkv = gkv + shift(key_parts[block], "y", step).astype(F32)
    gq_rows = (gq * FACTOR).T
    gq_sum = gq_rows[:PAIR] + shift(gq_rows[PAIR:].astype(BF16), "x_lo", 1).astype(F32)
    grads = jnp.concatenate([gq_sum.astype(BF16), gkv.astype(BF16)], axis=1)
    mine, back = grads[:ROWS], shift(grads[ROWS:], "core", 1)

    def columns(i):
        a, b = mine[:, i * HD : (i + 1) * HD], back[:, i * HD : (i + 1) * HD]
        return jnp.where(core == 0, jnp.concatenate([a, b], axis=1), jnp.concatenate([b, a], axis=1))

    return columns(0), columns(1), columns(2), grad_out_weight


def solution(mesh):
    devices = mesh.devices.reshape(NY, 2, 2, 2, NZ)
    fine = Mesh(devices, ("y", "x_lo", "core", "x_hi", "z"))
    ctx, head = ("y", "x_lo", "core"), ("x_hi", "z")
    return jax.shard_map(
        on_device,
        mesh=fine,
        in_specs=(
            P(ctx, head),
            P(ctx, head),
            P(ctx, head),
            P(ctx, head),
            P(head, None),
            P(),
            P(ctx),
        ),
        out_specs=(P(ctx, head), P(ctx, head), P(ctx, head), P(head, ctx)),
        check_vma=False,
    )
```

```python
import math

import jax
import jax.numpy as jnp
from jax import lax
from jax.experimental import pallas as pl
from jax.experimental.pallas import tpu as pltpu
from jax.sharding import Mesh, PartitionSpec as P

ROWS = 320
PAIR = 640
HD = 128
NQ = 1280
COLS = 256
FACTOR = HD ** -0.5
SCALE2 = FACTOR * math.log2(math.e)
FLOOR = -1e30
BIG = 1e37
NY = 4
NZ = 8

F32 = jnp.float32
BF16 = jnp.bfloat16

NT = (((1,), (1,)), ((), ()))
NN = (((1,), (0,)), ((), ()))
TN = (((0,), (0,)), ((), ()))


def dot(a, b, dims):
    return lax.dot_general(a, b, dims, preferred_element_type=F32)


BLOCK_Y = (0, NY - 1, 1, 2)


def doc_of(pos, lengths):
    total, end = jnp.zeros_like(pos), 0
    for i in range(8):
        end = end + lengths[i]
        total = total + jnp.where(pos >= end, 1, 0)
    return total


def token_of(base, row):
    turned = row + lax.axis_index("core") * ROWS
    return base + jnp.where(turned >= PAIR, turned - PAIR, turned)


def key_base(block):
    return lax.rem(lax.axis_index("y") + BLOCK_Y[block], NY) * NQ + lax.axis_index("x_lo") * PAIR


def on_visible(block, lengths, run):
    qb, kb = lax.axis_index("y") * NQ, key_base(block)
    q_low, q_high = doc_of(qb, lengths), doc_of(qb + NQ - 1, lengths)
    k_low, k_high = doc_of(kb, lengths), doc_of(kb + PAIR - 1, lengths)
    pl.when((q_high >= k_low) & (k_high >= q_low))(run)


def own_docs(base, lengths):
    row = lax.broadcasted_iota(jnp.int32, (PAIR, HD), 0)
    column = lax.broadcasted_iota(jnp.int32, (PAIR, HD), 1)
    return doc_of(token_of(base, row), lengths) == column, column < 8


def fill_keys(wide, kv_ref, block, lengths):
    own, _ = own_docs(key_base(block), lengths)
    wide[:, :HD] = kv_ref[:, :HD]
    wide[:, HD:] = jnp.where(own, 1.0, 0.0).astype(BF16)


def fill_queries(wide, queries, lengths):
    for half, (here, q_ref) in enumerate(zip(HALVES, queries)):
        base = lax.axis_index("y") * NQ + jnp.where(lax.axis_index("x_lo") == half, 0, PAIR)
        own, listed = own_docs(base, lengths)
        wide[here, :HD] = q_ref[...]
        wide[here, HD:] = jnp.where(listed & jnp.logical_not(own), -BIG, 0.0).astype(BF16)


def columns_of(core):
    return pl.ds(pl.multiple_of(core * HD, HD), HD)


HALVES = (slice(0, PAIR), slice(PAIR, NQ))


def split_kernel(q_ref, k_ref, v_ref, send_ref):
    there = columns_of(1 - lax.axis_index("core"))
    for i, ref in enumerate((k_ref, v_ref, q_ref)):
        send_ref[:, i * HD : (i + 1) * HD] = ref[:, there]


def join_kernel(q_ref, k_ref, v_ref, back_ref, near_ref, far_ref, kv_ref, own_ref, ring_ref):
    here = columns_of(lax.axis_index("core"))
    kv_ref[:ROWS, :HD] = k_ref[:, here]
    kv_ref[:ROWS, HD:] = v_ref[:, here]
    own_ref[:ROWS, :] = q_ref[:, here]
    kv_ref[ROWS:, :] = back_ref[:, : 2 * HD]
    own_ref[ROWS:, :] = back_ref[:, 2 * HD :]
    ring_ref[:ROWS, :] = near_ref[...]
    ring_ref[ROWS:, :] = far_ref[...]


def forward_kernel(lengths, q_own, q_far, kv0, kv1, kv2, kv3, after_up, after_down, out_ref, wide_q, wide_k, acc, m_ref, l_ref):
    fill_queries(wide_q, (q_own, q_far), lengths)
    acc[...] = jnp.zeros_like(acc)
    m_ref[...] = jnp.full_like(m_ref, FLOOR)
    l_ref[...] = jnp.zeros_like(l_ref)
    for block, kv_ref in enumerate((kv0, kv1, kv2, kv3)):

        def run(block=block, kv_ref=kv_ref):
            fill_keys(wide_k, kv_ref, block, lengths)
            for here in HALVES:
                s = dot(wide_k[...], wide_q[here, :], NT) * SCALE2
                old = m_ref[:, here]
                new = jnp.maximum(old, jnp.max(s, axis=0, keepdims=True))
                p = jnp.exp2(s - new)
                shrink = jnp.exp2(old - new)
                m_ref[:, here] = new
                l_ref[:, here] = l_ref[:, here] * shrink + jnp.sum(p, axis=0, keepdims=True)
                acc[:, here] = acc[:, here] * shrink + dot(kv_ref[:, HD:], p.astype(BF16), TN)

        on_visible(block, lengths, run)
    total = l_ref[...]
    seen = total > 0
    safe = jnp.where(seen, total, 1.0)
    out_ref[:HD, :] = (acc[...] / safe).astype(BF16)
    rest = jnp.where(seen, m_ref[...] + jnp.log2(safe), FLOOR)
    parts = []
    for _ in range(3):
        part = rest.astype(BF16).astype(F32)
        parts.append(part)
        rest = rest - part
    parts.append(jnp.zeros((13, NQ), F32))
    out_ref[HD:, :] = jnp.concatenate(parts, axis=0).astype(BF16)


def merge_kernel(mine, theirs, att_ref, lse_ref, keep_ref, give_ref):
    def log_total(ref, columns):
        parts = ref[HD:, columns].astype(F32)
        return parts[0:1] + parts[1:2] + parts[2:3]

    for half in range(2):
        here, there = HALVES[half], HALVES[1 - half]
        a, b = log_total(mine, here), log_total(theirs, there)
        top = jnp.maximum(a, b)
        lse = top + jnp.log2(jnp.exp2(a - top) + jnp.exp2(b - top))
        lse_ref[:, here] = lse
        att = mine[:HD, here].astype(F32) * jnp.exp2(a - lse) + theirs[:HD, there].astype(F32) * jnp.exp2(b - lse)
        att = att.astype(BF16)
        att_ref[:, here] = att
        if half == 0:
            keep_ref[...] = att[:, :ROWS]
            give_ref[...] = att[:, ROWS:]


def pieces_of(refs):
    start, up1, down1, up2, down2, up3, down3, far_up, far_down = refs
    listed = []
    for ref, distance in zip((start, up1, down1, up2, down2, up3, down3), (0, 1, -1, 2, -2, 3, -3)):
        listed += [(ref, 0, 0, distance), (ref, ROWS, 1, distance)]
    listed += [(far_up, 0, 0, 4), (far_down, 0, 1, 4)]
    for ref, first, far, distance in listed:
        x_hi = lax.axis_index("x_hi")
        z = lax.rem(lax.axis_index("z") - distance + NZ, NZ)
        yield (1 - x_hi if far else x_hi), z, distance % 2, ref[first : first + ROWS, :]


def dout_kernel(w_hbm, after, *refs):
    pieces, (keep_ref, give_ref, w, acc, sem) = refs[:9], refs[9:]
    copy = pltpu.make_async_copy(w_hbm, w, sem)
    copy.start()
    copy.wait()
    total = jnp.zeros((ROWS, COLS), F32)
    for x_hi, z, _, piece in pieces_of(pieces):
        columns = pl.ds(pl.multiple_of((x_hi * NZ + z) * COLS, COLS), COLS)
        total = total + dot(piece, w[:, columns], NT)
    acc[...] = total
    core = lax.axis_index("core")
    keep_ref[...] = acc[:, columns_of(core)].astype(BF16)
    give_ref[...] = acc[:, columns_of(1 - core)].astype(BF16)


def weight_kernel(att_own, att_other, *refs):
    pieces, (keep_ref, give_ref, both) = refs[:9], refs[9:]
    core = lax.axis_index("core")
    both[columns_of(core), :] = att_own[...]
    both[columns_of(1 - core), :] = att_other[...]
    y, x_lo = lax.axis_index("y"), lax.axis_index("x_lo")

    def run(same, other):
        for x_hi, z, odd, piece in pieces_of(pieces):
            slot = lax.rem(x_hi * 2 + z // 4 - y + NY, NY) + jnp.where(lax.rem(z // 2, 2) == x_lo, 0, NY)
            (other if odd else same)[slot] = dot(both[...], piece, NN).astype(BF16)

    alike = lax.rem(lax.axis_index("z"), 2) == core
    pl.when(alike)(lambda: run(keep_ref, give_ref))
    pl.when(jnp.logical_not(alike))(lambda: run(give_ref, keep_ref))


def chip_sum_kernel(keep, back, own_ref, send_ref):
    own_ref[...] = keep[:NY].astype(F32) + back[:NY].astype(F32)
    send_ref[...] = (keep[NY:].astype(F32) + back[NY:].astype(F32)).astype(BF16)


def pair_sum_kernel(own, back, own_ref, *send_refs):
    own_ref[...] = own[0] + back[0].astype(F32)
    for i, ref in enumerate(send_refs):
        ref[...] = (own[i + 1] + back[i + 1].astype(F32)).astype(BF16)


def backward_kernel(lengths, *refs):
    queries, dos, (lse_ref, att_ref), kvs, refs = refs[:2], refs[2:6], refs[6:8], refs[8:12], refs[13:]
    gq_keep, gq_give = refs[:2]
    gkv_refs = refs[2:6]
    gq_ref, grad_out, row_dot, probs, scores, wide_q, wide_k = refs[6:]
    fill_queries(wide_q, queries, lengths)
    for i, ref in enumerate(dos):
        grad_out[i * ROWS : (i + 1) * ROWS, :] = ref[...]
    for here in HALVES:
        turned = grad_out[here, :].astype(F32).T
        row_dot[:, here] = jnp.sum(turned * att_ref[:, here].astype(F32), axis=0, keepdims=True)
    gq_ref[...] = jnp.zeros_like(gq_ref)
    for block, (kv_ref, gkv_ref) in enumerate(zip(kvs, gkv_refs)):
        gkv_ref[...] = jnp.zeros_like(gkv_ref)

        def run(block=block, kv_ref=kv_ref, gkv_ref=gkv_ref):
            fill_keys(wide_k, kv_ref, block, lengths)
            keys = kv_ref[:, :HD]
            vals = kv_ref[:, HD:]
            gk = jnp.zeros((PAIR, HD), F32)
            gv = jnp.zeros((PAIR, HD), F32)
            for half, here in enumerate(HALVES):
                grads = grad_out[here, :]
                s = dot(wide_k[...], wide_q[here, :], NT) * SCALE2 - lse_ref[:, here]
                p = jnp.exp2(s)
                probs[:, here] = p.astype(BF16)
                scores[:, here] = (p * (dot(vals, grads, NT) - row_dot[:, here])).astype(BF16)
                gv = gv + dot(probs[:, here], grads, NN)
                gk = gk + dot(scores[:, here], queries[half][...], NN)
            gq_ref[...] += dot(keys, scores[...], TN)
            gkv_ref[:, :HD] = (gk * FACTOR).astype(gkv_ref.dtype)
            gkv_ref[:, HD:] = gv.astype(gkv_ref.dtype)

        on_visible(block, lengths, run)
    gq_keep[...] = (gq_ref[:, :PAIR] * FACTOR).T
    gq_give[...] = (gq_ref[:, PAIR:] * FACTOR).T.astype(BF16)


def row_sum_kernel(gq, gq_back, gkv, back1, back2, back3, keep_ref, give_ref):
    for rows, ref in ((slice(0, ROWS), keep_ref), (slice(ROWS, PAIR), give_ref)):
        ref[:, :HD] = (gq[rows, :] + gq_back[rows, :].astype(F32)).astype(BF16)
        total = gkv[rows, :]
        for back in (back1, back2, back3):
            total = total + back[rows, :].astype(F32)
        ref[:, HD:] = total.astype(BF16)


def finish_kernel(keep, back, gq_ref, gk_ref, gv_ref):
    core = lax.axis_index("core")
    here, there = columns_of(core), columns_of(1 - core)
    for i, ref in enumerate((gq_ref, gk_ref, gv_ref)):
        ref[:, here] = keep[:, i * HD : (i + 1) * HD]
        ref[:, there] = back[:, i * HD : (i + 1) * HD]


def weight_sum_kernel(own, back1, back2, back3, out_ref):
    out_ref[...] = own[...] + back1[...].astype(F32) + back2[...].astype(F32) + back3[...].astype(F32)


SMEM = pl.BlockSpec(memory_space=pltpu.SMEM)
VMEM = pl.BlockSpec(memory_space=pltpu.VMEM)
ANY = pl.BlockSpec(memory_space=pl.ANY)


def call(kernel, name, arrays, outs, scratch=(), flops=1e6, specs=None, vmem=12):
    moved = sum(a.size * a.dtype.itemsize for a in arrays) + sum(math.prod(s) * jnp.dtype(t).itemsize for s, t in outs)
    return pl.pallas_call(
        kernel,
        name=name,
        out_shape=[jax.ShapeDtypeStruct(s, t) for s, t in outs],
        in_specs=specs or [VMEM] * len(arrays),
        out_specs=[VMEM] * len(outs),
        scratch_shapes=[pltpu.VMEM(*item) if isinstance(item, tuple) else item for item in scratch],
        cost_estimate=pl.CostEstimate(flops=int(flops), bytes_accessed=int(moved), transcendentals=0),
        compiler_params=pltpu.CompilerParams(vmem_limit_bytes=vmem * 1024 * 1024),
    )(*arrays)


def shift(x, axis, step):
    size = {"y": NY, "x_lo": 2, "core": 2, "x_hi": 2, "z": NZ}[axis]
    return lax.ppermute(x, axis, [(i, (i + step) % size) for i in range(size)])


def swap_both(x):
    return lax.ppermute(x, ("x_lo", "core"), [(i, 3 - i) for i in range(4)])


def on_device(queries, keys, values, out_grad, out_weight, doc_lengths, loss_numer):
    scaled = (out_grad.astype(F32) * (loss_numer.astype(F32) / 8.0)[:, None]).astype(BF16)
    scaled_far = shift(scaled, "x_hi", 1)
    (sent,) = call(split_kernel, "split", [queries, keys, values], [((ROWS, 3 * HD), BF16)])
    kv, q_own, ring = call(
        join_kernel,
        "join",
        [queries, keys, values, shift(sent, "core", 1), scaled, scaled_far],
        [((PAIR, 2 * HD), BF16), ((PAIR, HD), BF16), ((PAIR, COLS), BF16)],
    )

    up, down = [ring], [ring]
    for _ in range(3):
        up.append(shift(up[-1], "z", 1))
        down.append(shift(down[-1], "z", -1))
    pieces = [ring, up[1], down[1], up[2], down[2], up[3], down[3]]
    pieces += [shift(up[3][:ROWS], "z", 1), shift(down[3][ROWS:], "z", -1)]

    kvs = [kv, shift(kv, "y", 1), shift(kv, "y", -1), shift(kv, "y", 2)]
    q_far = shift(q_own, "x_lo", 1)
    wide = [((NQ, 2 * HD), BF16), ((PAIR, 2 * HD), BF16)]
    (out_part,) = call(
        forward_kernel,
        "forward",
        [doc_lengths, q_own, q_far] + kvs + [up[2], down[2]],
        [((HD + 16, NQ), BF16)],
        wide + [((HD, NQ), F32), ((1, NQ), F32), ((1, NQ), F32)],
        2 * 2 * NQ * 2 * NQ * HD * 2,
        [SMEM] + [VMEM] * 6 + [ANY] * 2,
        24,
    )
    att, lse, att_keep, att_give = call(
        merge_kernel,
        "merge",
        [out_part, shift(out_part, "x_lo", 1)],
        [((HD, NQ), BF16), ((1, NQ), F32), ((HD, ROWS), BF16), ((HD, ROWS), BF16)],
    )
    att_other = shift(att_give, "core", 1)

    gw_keep, gw_give = call(
        weight_kernel,
        "weight",
        [att_keep, att_other] + pieces,
        [((2 * NY, COLS, COLS), BF16), ((2 * NY, COLS, COLS), BF16)],
        [((COLS, ROWS), BF16)],
        2 * ROWS * 4096 * COLS,
        vmem=16,
    )
    gw_back = shift(gw_give, "core", 1)
    do_keep, do_give = call(
        dout_kernel,
        "dout",
        [out_weight, gw_keep] + pieces,
        [((ROWS, HD), BF16), ((ROWS, HD), BF16)],
        [((COLS, 4096), BF16), ((ROWS, COLS), F32), pltpu.SemaphoreType.DMA],
        2 * ROWS * 4096 * COLS,
        [ANY, ANY] + [VMEM] * 9,
        16,
    )
    dos = [do_keep, shift(do_give, "core", 1), shift(do_keep, "x_lo", 1), swap_both(do_give)]
    gw_own, gw_send = call(
        chip_sum_kernel, "chip_sum", [gw_keep, gw_back], [((NY, COLS, COLS), F32), ((NY, COLS, COLS), BF16)]
    )
    gw_far = shift(gw_send, "x_lo", 1)

    block = ((PAIR, 2 * HD), BF16)
    gq_keep, gq_give, part0, part1, part2, part3 = call(
        backward_kernel,
        "backward",
        [doc_lengths, q_own, q_far] + dos + [lse, att] + kvs + [gw_send],
        [((PAIR, HD), F32), ((PAIR, HD), BF16), ((PAIR, 2 * HD), F32), block, block, block],
        [((HD, NQ), F32), ((NQ, HD), BF16), ((1, NQ), F32), ((PAIR, NQ), BF16), ((PAIR, NQ), BF16)] + wide,
        2 * 5 * NQ * 2 * NQ * HD * 2,
        [SMEM] + [VMEM] * 12 + [ANY],
        32,
    )
    backs = [shift(part3, "y", 2), shift(part1, "y", -1), shift(part2, "y", 1)]
    gq_back = shift(gq_give, "x_lo", 1)
    gw_parts = call(pair_sum_kernel, "pair_sum", [gw_own, gw_far], [((COLS, COLS), F32)] + [((COLS, COLS), BF16)] * 3)
    gw_backs = [shift(gw_parts[step], "y", step) for step in (1, 2, 3)]
    keep, give = call(
        row_sum_kernel,
        "row_sum",
        [gq_keep, gq_back, part0] + backs,
        [((ROWS, 3 * HD), BF16), ((ROWS, 3 * HD), BF16)],
    )
    (grad_out_weight,) = call(weight_sum_kernel, "weight_sum", [gw_parts[0]] + gw_backs, [((COLS, COLS), F32)])
    grad_queries, grad_keys, grad_values = call(
        finish_kernel, "finish", [keep, shift(give, "core", 1)], [((ROWS, COLS), BF16)] * 3
    )
    return grad_queries, grad_keys, grad_values, grad_out_weight


def solution(mesh):
    devices = mesh.devices.reshape(NY, 2, 2, 2, NZ)
    fine = Mesh(devices, ("y", "x_lo", "core", "x_hi", "z"))
    ctx, head = ("y", "x_lo", "core"), ("x_hi", "z")
    return jax.shard_map(
        on_device,
        mesh=fine,
        in_specs=(
            P(ctx, head),
            P(ctx, head),
            P(ctx, head),
            P(ctx, head),
            P(head, None),
            P(),
            P(ctx),
        ),
        out_specs=(P(ctx, head), P(ctx, head), P(ctx, head), P(head, ctx)),
        check_vma=False,
    )
```

```python
import functools
import math

import jax
import jax.numpy as jnp
from jax import lax
from jax.experimental import pallas as pl
from jax.experimental.pallas import tpu as pltpu
from jax.sharding import Mesh, PartitionSpec as P

ROWS = 320
PAIR = 640
HD = 128
NQ = 1280
COLS = 256
FACTOR = HD ** -0.5
SCALE2 = FACTOR * math.log2(math.e)
FLOOR = -1e30
BIG = 1e37
NY = 4
NZ = 8

F32 = jnp.float32
BF16 = jnp.bfloat16

NT = (((1,), (1,)), ((), ()))
NN = (((1,), (0,)), ((), ()))
TN = (((0,), (0,)), ((), ()))


def dot(a, b, dims):
    return lax.dot_general(a, b, dims, preferred_element_type=F32)


BLOCK_Y = (0, NY - 1, 1, 2)


def token_of(base, row):
    turned = row + lax.axis_index("core") * ROWS
    return base + jnp.where(turned >= PAIR, turned - PAIR, turned)


def key_base(block):
    return lax.rem(lax.axis_index("y") + BLOCK_Y[block], NY) * NQ + lax.axis_index("x_lo") * PAIR


def own_docs(base, lengths):
    column = lax.broadcasted_iota(jnp.int32, (1, HD), 1)
    first, last = jnp.zeros((1, HD), jnp.int32), jnp.zeros((1, HD), jnp.int32)
    start = 0
    for i in range(8):
        first = jnp.where(column == i, start, first)
        start = start + lengths[i]
        last = jnp.where(column == i, start, last)
    token = token_of(base, lax.broadcasted_iota(jnp.int32, (PAIR, HD), 0))
    return (token >= first) & (token < last), column < 8


def fill_keys(wide, kv_ref, block, lengths):
    own, _ = own_docs(key_base(block), lengths)
    wide[:, :HD] = kv_ref[:, :HD]
    wide[:, HD:] = jnp.where(own, 1.0, 0.0).astype(BF16)


def fill_queries(wide, queries, lengths):
    for half, (here, q_ref) in enumerate(zip(HALVES, queries)):
        base = lax.axis_index("y") * NQ + jnp.where(lax.axis_index("x_lo") == half, 0, PAIR)
        own, listed = own_docs(base, lengths)
        wide[here, :HD] = q_ref[...]
        wide[here, HD:] = jnp.where(own, 0.0, jnp.where(listed, -BIG, 0.0)).astype(BF16)


def columns_of(core):
    return pl.ds(pl.multiple_of(core * HD, HD), HD)


HALVES = (slice(0, PAIR), slice(PAIR, NQ))


def join_kernel(held_ref, back_ref, kv_ref, own_ref):
    for rows, ref in ((slice(0, ROWS), held_ref), (slice(ROWS, PAIR), back_ref)):
        kv_ref[rows, :] = ref[:, : 2 * HD]
        own_ref[rows, :] = ref[:, 2 * HD :]


def stack_kernel(parts, *refs):
    out_ref, first = refs[-1], 0
    for ref, (start, count) in zip(refs[:-1], parts):
        out_ref[first : first + count, :] = ref[start : start + count, :]
        first += count


def forward_step(blocks, lengths, wide_q, wide_k, kvs, before, after, probs):
    for block, kv_ref, wide in zip(blocks, kvs, wide_k):
        fill_keys(wide, kv_ref, block, lengths)
    acc_in, m_in, l_in = before
    acc, m_ref, l_ref = after
    for here in HALVES:
        scores = [dot(wide[...], wide_q[here, :], NT) * SCALE2 for wide in wide_k]
        new = m_in[:, here]
        for s in scores:
            new = jnp.maximum(new, jnp.max(s, axis=0, keepdims=True))
        shrink = jnp.exp2(m_in[:, here] - new)
        total, out = l_in[:, here] * shrink, acc_in[:, here] * shrink
        for s, kv_ref, prob_ref in zip(scores, kvs, probs):
            p = jnp.exp2(s - new)
            total = total + jnp.sum(p, axis=0, keepdims=True)
            prob_ref[:, here] = p.astype(BF16)
            out = out + dot(kv_ref[:, HD:], prob_ref[:, here], TN)
        m_ref[:, here], l_ref[:, here], acc[:, here] = new, total, out


def forward_own_kernel(lengths, q_own, q_far, kv, wide_q, acc, m_ref, l_ref, prob, wide_k, acc0, m0, l0):
    fill_queries(wide_q, (q_own, q_far), lengths)
    acc0[...] = jnp.zeros_like(acc0)
    m0[...] = jnp.full_like(m0, FLOOR)
    l0[...] = jnp.zeros_like(l0)
    forward_step((0,), lengths, wide_q, (wide_k,), (kv,), (acc0, m0, l0), (acc, m_ref, l_ref), (prob,))


def forward_near_kernel(lengths, wide_q, kv1, kv2, acc0, m0, l0, acc, m_ref, l_ref, prob1, prob2, wide1, wide2):
    forward_step((1, 2), lengths, wide_q, (wide1, wide2), (kv1, kv2), (acc0, m0, l0), (acc, m_ref, l_ref), (prob1, prob2))


def forward_far_kernel(lengths, wide_q, kv, acc0, m0, l0, out_ref, m_ref, prob, wide_k, acc, l_ref):
    forward_step((3,), lengths, wide_q, (wide_k,), (kv,), (acc0, m0, l0), (acc, m_ref, l_ref), (prob,))
    total = l_ref[...]
    seen = total > 0
    safe = jnp.where(seen, total, 1.0)
    out_ref[:HD, :] = (acc[...] / safe).astype(BF16)
    rest = jnp.where(seen, m_ref[...] + jnp.log2(safe), FLOOR)
    parts = []
    for _ in range(3):
        part = rest.astype(BF16).astype(F32)
        parts.append(part)
        rest = rest - part
    parts.append(jnp.zeros((13, NQ), F32))
    out_ref[HD:, :] = jnp.concatenate(parts, axis=0).astype(BF16)


def merge_kernel(mine, theirs, att_ref, lse_ref, keep_ref, give_ref):
    def log_total(ref, columns):
        parts = ref[HD:, columns].astype(F32)
        return parts[0:1] + parts[1:2] + parts[2:3]

    for half in range(2):
        here, there = HALVES[half], HALVES[1 - half]
        a, b = log_total(mine, here), log_total(theirs, there)
        top = jnp.maximum(a, b)
        lse = top + jnp.log2(jnp.exp2(a - top) + jnp.exp2(b - top))
        lse_ref[:, here] = lse
        att = mine[:HD, here].astype(F32) * jnp.exp2(a - lse) + theirs[:HD, there].astype(F32) * jnp.exp2(b - lse)
        att = att.astype(BF16)
        att_ref[:, here] = att
        if half == 0:
            keep_ref[...] = att[:, :ROWS]
            give_ref[...] = att[:, ROWS:]


NEAR = ((0, 0, 0), (1, 0, ROWS), (-1, 0, 2 * ROWS), (2, 1, 0), (-2, 1, ROWS), (3, 2, 0), (-3, 3, 0), (4, 4, 0))
FAR = ((0, 5, 0), (1, 5, ROWS), (-1, 5, 2 * ROWS), (2, 6, 0), (-2, 6, ROWS), (3, 7, ROWS // 2), (-3, 8, ROWS // 2), (4, 9, 0))


def pieces_of(refs):
    own = lax.axis_index("x_hi")
    for x_hi, listed in ((own, NEAR), (1 - own, FAR)):
        for distance, i, first in listed:
            z = lax.rem(lax.axis_index("z") - distance + NZ, NZ)
            yield x_hi, z, distance % 2, refs[i][first : first + ROWS, :]


def dout_kernel(w_hbm, *refs):
    pieces, (keep_ref, give_ref, w, acc, sem) = refs[:10], refs[10:]
    copy = pltpu.make_async_copy(w_hbm, w, sem)
    copy.start()
    copy.wait()
    total = jnp.zeros((ROWS, COLS), F32)
    for x_hi, z, _, piece in pieces_of(pieces):
        columns = pl.ds(pl.multiple_of((x_hi * NZ + z) * COLS, COLS), COLS)
        total = total + dot(piece, w[:, columns], NT)
    acc[...] = total
    core = lax.axis_index("core")
    keep_ref[...] = acc[:, columns_of(core)].astype(BF16)
    give_ref[...] = acc[:, columns_of(1 - core)].astype(BF16)


def weight_kernel(att_own, att_other, *refs):
    pieces, (keep_ref, give_ref, both) = refs[:10], refs[10:]
    core = lax.axis_index("core")
    both[columns_of(core), :] = att_own[...]
    both[columns_of(1 - core), :] = att_other[...]
    y, x_lo = lax.axis_index("y"), lax.axis_index("x_lo")

    def run(same, other):
        for x_hi, z, odd, piece in pieces_of(pieces):
            first = jnp.where(lax.rem(z // 2, 2) == x_lo, 0, COLS)
            rows = pl.ds(pl.multiple_of(first, COLS), COLS)
            (other if odd else same)[lax.rem(x_hi * 2 + z // 4 - y + NY, NY), rows, :] = dot(both[...], piece, NN).astype(BF16)

    alike = lax.rem(lax.axis_index("z"), 2) == core
    pl.when(alike)(lambda: run(keep_ref, give_ref))
    pl.when(jnp.logical_not(alike))(lambda: run(give_ref, keep_ref))


def chip_sum_kernel(keep, back, own_ref, *send_refs):
    own_ref[...] = keep[0].astype(F32) + back[0].astype(F32)
    for i, ref in enumerate(send_refs):
        ref[...] = (keep[i + 1].astype(F32) + back[i + 1].astype(F32)).astype(BF16)


def row_pair_kernel(own, back1, back2, back3, own_ref, send_ref):
    for rows, ref in ((slice(0, COLS), own_ref), (slice(COLS, 2 * COLS), send_ref)):
        total = own[rows, :]
        for back in (back1, back2, back3):
            total = total + back[rows, :].astype(F32)
        ref[...] = total.astype(ref.dtype)


def backward_step(queries, grad_out, row_dot, lse_ref, gq_ref, m_ref, kvs, probs, gkv_refs, scratch):
    prob, score = scratch
    scale = jnp.exp2(m_ref[...] - lse_ref[...])
    for kv_ref, kept, gkv_ref in zip(kvs, probs, gkv_refs):
        keys, vals = kv_ref[:, :HD], kv_ref[:, HD:]
        gk = jnp.zeros((PAIR, HD), F32)
        for here, q_ref in zip(HALVES, queries):
            p = kept[:, here].astype(F32) * scale[:, here]
            prob[:, here] = p.astype(BF16)
            score[:, here] = (p * (dot(vals, grad_out[here, :], NT) - row_dot[:, here])).astype(BF16)
            gk = gk + dot(score[:, here], q_ref[...], NN)
        gq_ref[...] += dot(keys, score[...], TN)
        gkv_ref[:, :HD] = (gk * FACTOR).astype(gkv_ref.dtype)
        gkv_ref[:, HD:] = dot(prob[...], grad_out[...], NN).astype(gkv_ref.dtype)


def backward_far_kernel(
    q_own, q_far, do0, do1, do2, do3, lse_ref, att_ref, m_ref, kv, kept, gq_ref, grad_out, row_dot, gkv_ref, *scratch
):
    for i, ref in enumerate((do0, do1, do2, do3)):
        grad_out[i * ROWS : (i + 1) * ROWS, :] = ref[...]
    for here in HALVES:
        turned = grad_out[here, :].astype(F32).T
        row_dot[:, here] = jnp.sum(turned * att_ref[:, here].astype(F32), axis=0, keepdims=True)
    gq_ref[...] = jnp.zeros_like(gq_ref)
    backward_step((q_own, q_far), grad_out, row_dot, lse_ref, gq_ref, m_ref, (kv,), (kept,), (gkv_ref,), scratch)


def backward_near_kernel(
    q_own, q_far, grad_out, row_dot, lse_ref, m_ref, kv1, kv2, kept1, kept2, gq_in, gq_ref, gkv1, gkv2, *scratch
):
    gq_ref[...] = gq_in[...]
    backward_step(
        (q_own, q_far), grad_out, row_dot, lse_ref, gq_ref, m_ref, (kv1, kv2), (kept1, kept2), (gkv1, gkv2), scratch
    )


def backward_own_kernel(
    q_own, q_far, grad_out, row_dot, lse_ref, m_ref, kv, kept, gq_in, gq_keep, gq_give, gkv_ref, gq_ref, *scratch
):
    gq_ref[...] = gq_in[...]
    backward_step((q_own, q_far), grad_out, row_dot, lse_ref, gq_ref, m_ref, (kv,), (kept,), (gkv_ref,), scratch)
    gq_keep[...] = (gq_ref[:, :PAIR] * FACTOR).T
    gq_give[...] = (gq_ref[:, PAIR:] * FACTOR).T.astype(BF16)


def row_sum_kernel(gq, gq_back, gkv, back1, back2, back3, keep_ref, give_ref):
    for rows, ref in ((slice(0, ROWS), keep_ref), (slice(ROWS, PAIR), give_ref)):
        ref[:, :HD] = (gq[rows, :] + gq_back[rows, :].astype(F32)).astype(BF16)
        total = gkv[rows, :]
        for back in (back1, back2, back3):
            total = total + back[rows, :].astype(F32)
        ref[:, HD:] = total.astype(BF16)


def finish_kernel(keep, back, gq_ref, gk_ref, gv_ref):
    core = lax.axis_index("core")
    here, there = columns_of(core), columns_of(1 - core)
    for i, ref in enumerate((gq_ref, gk_ref, gv_ref)):
        ref[:, here] = keep[:, i * HD : (i + 1) * HD]
        ref[:, there] = back[:, i * HD : (i + 1) * HD]


def weight_sum_kernel(own, back, out_ref):
    out_ref[...] = own[...] + back[...].astype(F32)


SMEM = pl.BlockSpec(memory_space=pltpu.SMEM)
VMEM = pl.BlockSpec(memory_space=pltpu.VMEM)
ANY = pl.BlockSpec(memory_space=pl.ANY)


def call(kernel, name, arrays, outs, scratch=(), flops=1e6, specs=None, vmem=12, after=()):
    moved = sum(a.size * a.dtype.itemsize for a in arrays) + sum(math.prod(s) * jnp.dtype(t).itemsize for s, t in outs)
    count, arrays, specs = len(arrays), list(arrays), specs or [VMEM] * len(arrays)

    def body(*refs):
        kernel(*refs[:count], *refs[count + len(after) :])

    return pl.pallas_call(
        body,
        name=name,
        out_shape=[jax.ShapeDtypeStruct(s, t) for s, t in outs],
        in_specs=specs + [ANY] * len(after),
        out_specs=[VMEM] * len(outs),
        scratch_shapes=[pltpu.VMEM(*item) if isinstance(item, tuple) else item for item in scratch],
        cost_estimate=pl.CostEstimate(flops=int(flops), bytes_accessed=int(moved), transcendentals=0),
        compiler_params=pltpu.CompilerParams(vmem_limit_bytes=vmem * 1024 * 1024),
    )(*arrays, *after)


def shift(x, axis, step):
    size = {"y": NY, "x_lo": 2, "core": 2, "x_hi": 2, "z": NZ}[axis]
    return lax.ppermute(x, axis, [(i, (i + step) % size) for i in range(size)])


def swap_both(x):
    return lax.ppermute(x, ("x_lo", "core"), [(i, 3 - i) for i in range(4)])


def stack(*parts, after=()):
    parts = [part if isinstance(part, tuple) else (part, 0, part.shape[0]) for part in parts]
    ranges = [(first, count) for _, first, count in parts]
    rows = sum(count for _, count in ranges)
    return call(functools.partial(stack_kernel, ranges), "stack", [p[0] for p in parts], [((rows, COLS), BF16)], after=after)[0]


def on_device(queries, keys, values, out_grad, out_weight, doc_lengths, loss_numer):
    scaled = (out_grad.astype(F32) * (loss_numer.astype(F32) / 8.0)[:, None]).astype(BF16)

    core = lax.axis_index("core")
    held, sent = (
        jnp.concatenate([lax.dynamic_slice_in_dim(a, which * HD, HD, 1) for a in (keys, values, queries)], axis=1)
        for which in (core, 1 - core)
    )
    kv, q_own = call(join_kernel, "join", [held, shift(sent, "core", 1)], [((PAIR, 2 * HD), BF16), ((PAIR, HD), BF16)])
    kvs = [kv, shift(kv, "y", 1), shift(kv, "y", -1), shift(kv, "y", 2)]
    q_far = shift(q_own, "x_lo", 1)

    up, down = [scaled], [scaled]
    for _ in range(3):
        up.append(shift(up[-1], "z", 1))
        down.append(shift(down[-1], "z", -1))
    half = ROWS // 2
    near = [stack(scaled, up[1], down[1], after=[]), stack(up[2], down[2], after=[kvs[3]])]
    far = [shift(a, "x_hi", 1) for a in near]
    up_last = shift(stack((up[3], 0, half), (far[1], 0, ROWS)), "z", 1)
    down_last = shift(stack((down[3], half, half), (far[1], ROWS, ROWS)), "z", -1)
    last = stack((up_last, 0, half), (down_last, 0, half))
    pieces = near + [up[3], down[3], last] + far + [up_last, down_last, shift(last, "x_hi", 1)]

    wide_q_kind, wide_k_kind = ((NQ, 2 * HD), BF16), ((PAIR, 2 * HD), BF16)
    acc_kind, row_kind, prob_kind = ((HD, NQ), F32), ((1, NQ), F32), ((PAIR, NQ), BF16)
    flops = 2 * 2 * NQ * PAIR * HD * 2
    wide_q, acc, m0, total, prob0 = call(
        forward_own_kernel,
        "forward_own",
        [doc_lengths, q_own, q_far, kvs[0]],
        [wide_q_kind, acc_kind, row_kind, row_kind, prob_kind],
        [wide_k_kind, acc_kind, row_kind, row_kind],
        flops,
        [SMEM] + [VMEM] * 3,
        16,
        after=[],
    )
    acc, m1, total, prob1, prob2 = call(
        forward_near_kernel,
        "forward_near",
        [doc_lengths, wide_q, kvs[1], kvs[2], acc, m0, total],
        [acc_kind, row_kind, row_kind, prob_kind, prob_kind],
        [wide_k_kind, wide_k_kind],
        2 * flops,
        [SMEM] + [VMEM] * 6,
        24,
        after=[],
    )
    out_part, m3, prob3 = call(
        forward_far_kernel,
        "forward_far",
        [doc_lengths, wide_q, kvs[3], acc, m1, total],
        [((HD + 16, NQ), BF16), row_kind, prob_kind],
        [wide_k_kind, acc_kind, row_kind],
        flops,
        [SMEM] + [VMEM] * 5,
        16,
        after=[far[1]],
    )
    att, lse, att_keep, att_give = call(
        merge_kernel,
        "merge",
        [out_part, shift(out_part, "x_lo", 1)],
        [((HD, NQ), BF16), row_kind, ((HD, ROWS), BF16), ((HD, ROWS), BF16)],
        after=[],
    )
    att_other = shift(att_give, "core", 1)

    do_keep, do_give = call(
        dout_kernel,
        "dout",
        [out_weight] + pieces,
        [((ROWS, HD), BF16), ((ROWS, HD), BF16)],
        [((COLS, 4096), BF16), ((ROWS, COLS), F32), pltpu.SemaphoreType.DMA],
        2 * ROWS * 4096 * COLS,
        [ANY] + [VMEM] * 10,
    )
    dos = [do_keep, shift(do_give, "core", 1), shift(do_keep, "x_lo", 1), swap_both(do_give)]

    gw_keep, gw_give = call(
        weight_kernel,
        "weight",
        [att_keep, att_other] + pieces,
        [((NY, 2 * COLS, COLS), BF16), ((NY, 2 * COLS, COLS), BF16)],
        [((COLS, ROWS), BF16)],
        2 * ROWS * 4096 * COLS,
        [VMEM] * 12,
    )
    gw_back = shift(gw_give, "core", 1)

    gw0, gw1, gw2, gw3 = call(
        chip_sum_kernel, "chip_sum", [gw_keep, gw_back], [((2 * COLS, COLS), F32)] + [((2 * COLS, COLS), BF16)] * 3
    )
    gw_rows = [shift(gw1, "y", 1), shift(gw2, "y", 2), shift(gw3, "y", 3)]

    block = ((PAIR, 2 * HD), BF16)
    scratch = [prob_kind, prob_kind]
    flops = 2 * NQ * PAIR * HD
    gq, grad_out, row_dot, part3 = call(
        backward_far_kernel,
        "backward_far",
        [q_own, q_far] + dos + [lse, att, m3, kvs[3], prob3],
        [acc_kind, ((NQ, HD), BF16), row_kind, block],
        scratch,
        flops,
        vmem=16,
        after=[gw1],
    )
    back3 = shift(part3, "y", 2)
    gq, part1, part2 = call(
        backward_near_kernel,
        "backward_near",
        [q_own, q_far, grad_out, row_dot, lse, m1, kvs[1], kvs[2], prob1, prob2, gq],
        [acc_kind, block, block],
        scratch,
        2 * flops,
        vmem=16,
    )
    backs = [shift(part1, "y", -1), shift(part2, "y", 1), back3]
    gw_pair, gw_send = call(
        row_pair_kernel, "row_pair", [gw0] + gw_rows, [((COLS, COLS), F32), ((COLS, COLS), BF16)]
    )
    gw_far = shift(gw_send, "x_lo", 1)
    gq_keep, gq_give, part0 = call(
        backward_own_kernel,
        "backward_own",
        [q_own, q_far, grad_out, row_dot, lse, m0, kvs[0], prob0, gq],
        [((PAIR, HD), F32), ((PAIR, HD), BF16), ((PAIR, 2 * HD), F32)],
        [acc_kind] + scratch,
        flops,
        vmem=16,
        after=[gw_pair, back3, gw_far],
    )
    gq_back = shift(gq_give, "x_lo", 1)
    (grad_out_weight,) = call(weight_sum_kernel, "weight_sum", [gw_pair, gw_far], [((COLS, COLS), F32)])
    keep, give = call(
        row_sum_kernel,
        "row_sum",
        [gq_keep, gq_back, part0] + backs,
        [((ROWS, 3 * HD), BF16), ((ROWS, 3 * HD), BF16)],
        after=[grad_out_weight],
    )
    grad_queries, grad_keys, grad_values = call(
        finish_kernel, "finish", [keep, shift(give, "core", 1)], [((ROWS, COLS), BF16)] * 3
    )
    return grad_queries, grad_keys, grad_values, grad_out_weight


def solution(mesh):
    devices = mesh.devices.reshape(NY, 2, 2, 2, NZ)
    fine = Mesh(devices, ("y", "x_lo", "core", "x_hi", "z"))
    ctx, head = ("y", "x_lo", "core"), ("x_hi", "z")
    return jax.shard_map(
        on_device,
        mesh=fine,
        in_specs=(
            P(ctx, head),
            P(ctx, head),
            P(ctx, head),
            P(ctx, head),
            P(head, None),
            P(),
            P(ctx),
        ),
        out_specs=(P(ctx, head), P(ctx, head), P(ctx, head), P(head, ctx)),
        check_vma=False,
    )
```

```python
import functools
import math

import jax
import jax.numpy as jnp
from jax import lax
from jax.experimental import pallas as pl
from jax.experimental.pallas import tpu as pltpu
from jax.sharding import Mesh, PartitionSpec as P

ROWS = 320
PAIR = 640
HD = 128
NQ = 1280
COLS = 256
FACTOR = HD ** -0.5
SCALE2 = FACTOR * math.log2(math.e)
FLOOR = -1e30
BIG = 1e37
NY = 4
NZ = 8

F32 = jnp.float32
BF16 = jnp.bfloat16

NT = (((1,), (1,)), ((), ()))
NN = (((1,), (0,)), ((), ()))
TN = (((0,), (0,)), ((), ()))


def dot(a, b, dims):
    return lax.dot_general(a, b, dims, preferred_element_type=F32)


BLOCK_Y = (0, NY - 1, 1, 2)


def token_of(base, row):
    turned = row + lax.axis_index("core") * ROWS
    return base + jnp.where(turned >= PAIR, turned - PAIR, turned)


def key_base(block):
    return lax.rem(lax.axis_index("y") + BLOCK_Y[block], NY) * NQ + lax.axis_index("x_lo") * PAIR


def own_docs(base, lengths):
    column = lax.broadcasted_iota(jnp.int32, (1, HD), 1)
    first, last = jnp.zeros((1, HD), jnp.int32), jnp.zeros((1, HD), jnp.int32)
    start = 0
    for i in range(8):
        first = jnp.where(column == i, start, first)
        start = start + lengths[i]
        last = jnp.where(column == i, start, last)
    token = token_of(base, lax.broadcasted_iota(jnp.int32, (PAIR, HD), 0))
    return (token >= first) & (token < last), column < 8


def fill_keys(wide, kv_ref, block, lengths):
    own, _ = own_docs(key_base(block), lengths)
    wide[:, :HD] = kv_ref[:, :HD]
    wide[:, HD:] = jnp.where(own, 1.0, 0.0).astype(BF16)


def fill_queries(wide, queries, lengths):
    for half, (here, q_ref) in enumerate(zip(HALVES, queries)):
        base = lax.axis_index("y") * NQ + jnp.where(lax.axis_index("x_lo") == half, 0, PAIR)
        own, listed = own_docs(base, lengths)
        wide[here, :HD] = q_ref[...]
        wide[here, HD:] = jnp.where(own, 0.0, jnp.where(listed, -BIG, 0.0)).astype(BF16)


def columns_of(core):
    return pl.ds(pl.multiple_of(core * HD, HD), HD)


HALVES = (slice(0, PAIR), slice(PAIR, NQ))


def join_kernel(held_ref, back_ref, kv_ref, own_ref):
    for rows, ref in ((slice(0, ROWS), held_ref), (slice(ROWS, PAIR), back_ref)):
        kv_ref[rows, :] = ref[:, : 2 * HD]
        own_ref[rows, :] = ref[:, 2 * HD :]


def stack_kernel(parts, *refs):
    out_ref, first = refs[-1], 0
    for ref, (start, count) in zip(refs[:-1], parts):
        out_ref[first : first + count, :] = ref[start : start + count, :]
        first += count


def forward_step(blocks, lengths, wide_q, wide_k, kvs, before, after, probs):
    for block, kv_ref, wide in zip(blocks, kvs, wide_k):
        fill_keys(wide, kv_ref, block, lengths)
    acc_in, m_in, l_in = before
    acc, m_ref, l_ref = after
    turned = [kv_ref[:, HD:].T for kv_ref in kvs]
    for here in (slice(0, 256), slice(256, 512), slice(512, 768), slice(768, 1024), slice(1024, NQ)):
        scores = [dot(wide[...], wide_q[here, :], NT) * SCALE2 for wide in wide_k]
        new = m_in[:, here]
        for s in scores:
            new = jnp.maximum(new, jnp.max(s, axis=0, keepdims=True))
        shrink = jnp.exp2(m_in[:, here] - new)
        total, out = l_in[:, here] * shrink, acc_in[:, here] * shrink
        for s, vals, prob_ref in zip(scores, turned, probs):
            p = jnp.exp2(s - new)
            total = total + jnp.sum(p, axis=0, keepdims=True)
            kept = p.astype(BF16)
            prob_ref[:, here] = kept
            out = out + dot(vals, kept, NN)
        m_ref[:, here], l_ref[:, here], acc[:, here] = new, total, out


def forward_own_kernel(lengths, q_own, q_far, kv, wide_q, acc, m_ref, l_ref, prob, wide_k, acc0, m0, l0):
    fill_queries(wide_q, (q_own, q_far), lengths)
    acc0[...] = jnp.zeros_like(acc0)
    m0[...] = jnp.full_like(m0, FLOOR)
    l0[...] = jnp.zeros_like(l0)
    forward_step((0,), lengths, wide_q, (wide_k,), (kv,), (acc0, m0, l0), (acc, m_ref, l_ref), (prob,))


def forward_near_kernel(lengths, wide_q, kv1, kv2, acc0, m0, l0, acc, m_ref, l_ref, prob1, prob2, wide1, wide2):
    forward_step((1, 2), lengths, wide_q, (wide1, wide2), (kv1, kv2), (acc0, m0, l0), (acc, m_ref, l_ref), (prob1, prob2))


def forward_far_kernel(lengths, wide_q, kv, acc0, m0, l0, out_ref, m_ref, prob, wide_k, acc, l_ref):
    forward_step((3,), lengths, wide_q, (wide_k,), (kv,), (acc0, m0, l0), (acc, m_ref, l_ref), (prob,))
    total = l_ref[...]
    seen = total > 0
    safe = jnp.where(seen, total, 1.0)
    out_ref[:HD, :] = (acc[...] * (1.0 / safe)).astype(BF16)
    rest = jnp.where(seen, m_ref[...] + jnp.log2(safe), FLOOR)
    parts = []
    for _ in range(3):
        part = rest.astype(BF16).astype(F32)
        parts.append(part)
        rest = rest - part
    parts.append(jnp.zeros((13, NQ), F32))
    out_ref[HD:, :] = jnp.concatenate(parts, axis=0).astype(BF16)


def merge_kernel(mine, theirs, att_ref, lse_ref, keep_ref, give_ref):
    def log_total(ref, columns):
        parts = ref[HD:, columns].astype(F32)
        return parts[0:1] + parts[1:2] + parts[2:3]

    for half in range(2):
        here, there = HALVES[half], HALVES[1 - half]
        a, b = log_total(mine, here), log_total(theirs, there)
        top = jnp.maximum(a, b)
        lse = top + jnp.log2(jnp.exp2(a - top) + jnp.exp2(b - top))
        lse_ref[:, here] = lse
        att = mine[:HD, here].astype(F32) * jnp.exp2(a - lse) + theirs[:HD, there].astype(F32) * jnp.exp2(b - lse)
        att = att.astype(BF16)
        att_ref[:, here] = att
        if half == 0:
            keep_ref[...] = att[:, :ROWS]
            give_ref[...] = att[:, ROWS:]


NEAR = ((0, 0, 0), (1, 0, ROWS), (-1, 0, 2 * ROWS), (2, 1, 0), (-2, 1, ROWS), (3, 2, 0), (-3, 3, 0), (4, 4, 0))
FAR = ((0, 5, 0), (1, 5, ROWS), (-1, 5, 2 * ROWS), (2, 6, 0), (-2, 6, ROWS), (3, 7, ROWS // 2), (-3, 8, ROWS // 2), (4, 9, 0))


def pieces_of(refs):
    own = lax.axis_index("x_hi")
    for x_hi, listed in ((own, NEAR), (1 - own, FAR)):
        for distance, i, first in listed:
            z = lax.rem(lax.axis_index("z") - distance + NZ, NZ)
            yield x_hi, z, distance % 2, refs[i][first : first + ROWS, :]


def dout_kernel(w_hbm, *refs):
    pieces, (keep_ref, give_ref, w, acc, sem) = refs[:10], refs[10:]
    copy = pltpu.make_async_copy(w_hbm, w, sem)
    copy.start()
    copy.wait()
    total = jnp.zeros((ROWS, COLS), F32)
    for x_hi, z, _, piece in pieces_of(pieces):
        columns = pl.ds(pl.multiple_of((x_hi * NZ + z) * COLS, COLS), COLS)
        total = total + dot(piece, w[:, columns], NT)
    acc[...] = total
    core = lax.axis_index("core")
    keep_ref[...] = acc[:, columns_of(core)].astype(BF16)
    give_ref[...] = acc[:, columns_of(1 - core)].astype(BF16)


def weight_kernel(att_own, att_other, *refs):
    pieces, (keep_ref, give_ref, both) = refs[:10], refs[10:]
    core = lax.axis_index("core")
    both[columns_of(core), :] = att_own[...]
    both[columns_of(1 - core), :] = att_other[...]
    y, x_lo = lax.axis_index("y"), lax.axis_index("x_lo")

    def run(same, other):
        for x_hi, z, odd, piece in pieces_of(pieces):
            first = jnp.where(lax.rem(z // 2, 2) == x_lo, 0, COLS)
            rows = pl.ds(pl.multiple_of(first, COLS), COLS)
            (other if odd else same)[lax.rem(x_hi * 2 + z // 4 - y + NY, NY), rows, :] = dot(both[...], piece, NN).astype(BF16)

    alike = lax.rem(lax.axis_index("z"), 2) == core
    pl.when(alike)(lambda: run(keep_ref, give_ref))
    pl.when(jnp.logical_not(alike))(lambda: run(give_ref, keep_ref))


def chip_sum_kernel(keep, back, own_ref, *send_refs):
    own_ref[...] = keep[0].astype(F32) + back[0].astype(F32)
    for i, ref in enumerate(send_refs):
        ref[...] = (keep[i + 1].astype(F32) + back[i + 1].astype(F32)).astype(BF16)


def row_pair_kernel(own, back1, back2, back3, own_ref, send_ref):
    for rows, ref in ((slice(0, COLS), own_ref), (slice(COLS, 2 * COLS), send_ref)):
        total = own[rows, :]
        for back in (back1, back2, back3):
            total = total + back[rows, :].astype(F32)
        ref[...] = total.astype(ref.dtype)


def backward_step(queries, grad_out, row_dot, lse_ref, gq_ref, m_ref, kvs, probs, gkv_refs, scratch):
    prob, score = scratch
    scale = jnp.exp2(m_ref[...] - lse_ref[...])
    for kv_ref, kept, gkv_ref in zip(kvs, probs, gkv_refs):
        keys, vals = kv_ref[:, :HD], kv_ref[:, HD:]
        gk = jnp.zeros((PAIR, HD), F32)
        for here, q_ref in zip(HALVES, queries):
            p = kept[:, here].astype(F32) * scale[:, here]
            prob[:, here] = p.astype(BF16)
            part = (p * (dot(vals, grad_out[here, :], NT) - row_dot[:, here])).astype(BF16)
            score[:, here] = part
            gk = gk + dot(part, q_ref[...], NN)
        gq_ref[...] += dot(keys, score[...], TN)
        gkv_ref[:, :HD] = (gk * FACTOR).astype(gkv_ref.dtype)
        gkv_ref[:, HD:] = dot(prob[...], grad_out[...], NN).astype(gkv_ref.dtype)


def backward_far_kernel(
    q_own, q_far, do0, do1, do2, do3, lse_ref, att_ref, m_ref, kv, kept, gq_ref, grad_out, row_dot, gkv_ref, *scratch
):
    for i, ref in enumerate((do0, do1, do2, do3)):
        grad_out[i * ROWS : (i + 1) * ROWS, :] = ref[...]
    for here in HALVES:
        turned = grad_out[here, :].astype(F32).T
        row_dot[:, here] = jnp.sum(turned * att_ref[:, here].astype(F32), axis=0, keepdims=True)
    gq_ref[...] = jnp.zeros_like(gq_ref)
    backward_step((q_own, q_far), grad_out, row_dot, lse_ref, gq_ref, m_ref, (kv,), (kept,), (gkv_ref,), scratch)


def backward_near_kernel(
    q_own, q_far, grad_out, row_dot, lse_ref, m_ref, kv1, kv2, kept1, kept2, gq_in, gq_ref, gkv1, gkv2, *scratch
):
    gq_ref[...] = gq_in[...]
    backward_step(
        (q_own, q_far), grad_out, row_dot, lse_ref, gq_ref, m_ref, (kv1, kv2), (kept1, kept2), (gkv1, gkv2), scratch
    )


def backward_own_kernel(
    q_own, q_far, grad_out, row_dot, lse_ref, m_ref, kv, kept, gq_in, gq_keep, gq_give, gkv_ref, gq_ref, *scratch
):
    gq_ref[...] = gq_in[...]
    backward_step((q_own, q_far), grad_out, row_dot, lse_ref, gq_ref, m_ref, (kv,), (kept,), (gkv_ref,), scratch)
    gq_keep[...] = (gq_ref[:, :PAIR] * FACTOR).T
    gq_give[...] = (gq_ref[:, PAIR:] * FACTOR).T.astype(BF16)


def row_sum_kernel(gq, gq_back, gkv, back1, back2, back3, keep_ref, give_ref):
    for rows, ref in ((slice(0, ROWS), keep_ref), (slice(ROWS, PAIR), give_ref)):
        ref[:, :HD] = (gq[rows, :] + gq_back[rows, :].astype(F32)).astype(BF16)
        total = gkv[rows, :]
        for back in (back1, back2, back3):
            total = total + back[rows, :].astype(F32)
        ref[:, HD:] = total.astype(BF16)


def finish_kernel(keep, back, gq_ref, gk_ref, gv_ref):
    core = lax.axis_index("core")
    here, there = columns_of(core), columns_of(1 - core)
    for i, ref in enumerate((gq_ref, gk_ref, gv_ref)):
        ref[:, here] = keep[:, i * HD : (i + 1) * HD]
        ref[:, there] = back[:, i * HD : (i + 1) * HD]


def weight_sum_kernel(own, back, out_ref):
    out_ref[...] = own[...] + back[...].astype(F32)


SMEM = pl.BlockSpec(memory_space=pltpu.SMEM)
VMEM = pl.BlockSpec(memory_space=pltpu.VMEM)
ANY = pl.BlockSpec(memory_space=pl.ANY)


def call(kernel, name, arrays, outs, scratch=(), flops=1e6, specs=None, vmem=12, after=()):
    moved = sum(a.size * a.dtype.itemsize for a in arrays) + sum(math.prod(s) * jnp.dtype(t).itemsize for s, t in outs)
    count, arrays, specs = len(arrays), list(arrays), specs or [VMEM] * len(arrays)

    def body(*refs):
        kernel(*refs[:count], *refs[count + len(after) :])

    return pl.pallas_call(
        body,
        name=name,
        out_shape=[jax.ShapeDtypeStruct(s, t) for s, t in outs],
        in_specs=specs + [ANY] * len(after),
        out_specs=[VMEM] * len(outs),
        scratch_shapes=[pltpu.VMEM(*item) if isinstance(item, tuple) else item for item in scratch],
        cost_estimate=pl.CostEstimate(flops=int(flops), bytes_accessed=int(moved), transcendentals=0),
        compiler_params=pltpu.CompilerParams(vmem_limit_bytes=vmem * 1024 * 1024),
    )(*arrays, *after)


def shift(x, axis, step):
    size = {"y": NY, "x_lo": 2, "core": 2, "x_hi": 2, "z": NZ}[axis]
    return lax.ppermute(x, axis, [(i, (i + step) % size) for i in range(size)])


def swap_both(x):
    return lax.ppermute(x, ("x_lo", "core"), [(i, 3 - i) for i in range(4)])


def stack(*parts, after=()):
    parts = [part if isinstance(part, tuple) else (part, 0, part.shape[0]) for part in parts]
    ranges = [(first, count) for _, first, count in parts]
    rows = sum(count for _, count in ranges)
    return call(functools.partial(stack_kernel, ranges), "stack", [p[0] for p in parts], [((rows, COLS), BF16)], after=after)[0]


def on_device(queries, keys, values, out_grad, out_weight, doc_lengths, loss_numer):
    scaled = (out_grad.astype(F32) * (loss_numer.astype(F32) / 8.0)[:, None]).astype(BF16)

    core = lax.axis_index("core")
    held, sent = (
        jnp.concatenate([lax.dynamic_slice_in_dim(a, which * HD, HD, 1) for a in (keys, values, queries)], axis=1)
        for which in (core, 1 - core)
    )
    kv, q_own = call(join_kernel, "join", [held, shift(sent, "core", 1)], [((PAIR, 2 * HD), BF16), ((PAIR, HD), BF16)])
    kvs = [kv, shift(kv, "y", 1), shift(kv, "y", -1), shift(kv, "y", 2)]
    q_far = shift(q_own, "x_lo", 1)

    up, down = [scaled], [scaled]
    for _ in range(3):
        up.append(shift(up[-1], "z", 1))
        down.append(shift(down[-1], "z", -1))
    half = ROWS // 2
    near = [stack(scaled, up[1], down[1], after=[]), stack(up[2], down[2], after=[kvs[3]])]
    far = [shift(a, "x_hi", 1) for a in near]
    up_last = shift(stack((up[3], 0, half), (far[1], 0, ROWS)), "z", 1)
    down_last = shift(stack((down[3], half, half), (far[1], ROWS, ROWS)), "z", -1)
    last = stack((up_last, 0, half), (down_last, 0, half))
    pieces = near + [up[3], down[3], last] + far + [up_last, down_last, shift(last, "x_hi", 1)]

    wide_q_kind, wide_k_kind = ((NQ, 2 * HD), BF16), ((PAIR, 2 * HD), BF16)
    acc_kind, row_kind, prob_kind = ((HD, NQ), F32), ((1, NQ), F32), ((PAIR, NQ), BF16)
    flops = 2 * 2 * NQ * PAIR * HD * 2
    wide_q, acc, m0, total, prob0 = call(
        forward_own_kernel,
        "forward_own",
        [doc_lengths, q_own, q_far, kvs[0]],
        [wide_q_kind, acc_kind, row_kind, row_kind, prob_kind],
        [wide_k_kind, acc_kind, row_kind, row_kind],
        flops,
        [SMEM] + [VMEM] * 3,
        16,
        after=[],
    )
    acc, m1, total, prob1, prob2 = call(
        forward_near_kernel,
        "forward_near",
        [doc_lengths, wide_q, kvs[1], kvs[2], acc, m0, total],
        [acc_kind, row_kind, row_kind, prob_kind, prob_kind],
        [wide_k_kind, wide_k_kind],
        2 * flops,
        [SMEM] + [VMEM] * 6,
        24,
        after=[],
    )
    out_part, m3, prob3 = call(
        forward_far_kernel,
        "forward_far",
        [doc_lengths, wide_q, kvs[3], acc, m1, total],
        [((HD + 16, NQ), BF16), row_kind, prob_kind],
        [wide_k_kind, acc_kind, row_kind],
        flops,
        [SMEM] + [VMEM] * 5,
        16,
        after=[far[1]],
    )
    att, lse, att_keep, att_give = call(
        merge_kernel,
        "merge",
        [out_part, shift(out_part, "x_lo", 1)],
        [((HD, NQ), BF16), row_kind, ((HD, ROWS), BF16), ((HD, ROWS), BF16)],
        after=[],
    )
    att_other = shift(att_give, "core", 1)

    do_keep, do_give = call(
        dout_kernel,
        "dout",
        [out_weight] + pieces,
        [((ROWS, HD), BF16), ((ROWS, HD), BF16)],
        [((COLS, 4096), BF16), ((ROWS, COLS), F32), pltpu.SemaphoreType.DMA],
        2 * ROWS * 4096 * COLS,
        [ANY] + [VMEM] * 10,
    )
    dos = [do_keep, shift(do_give, "core", 1), shift(do_keep, "x_lo", 1), swap_both(do_give)]

    gw_keep, gw_give = call(
        weight_kernel,
        "weight",
        [att_keep, att_other] + pieces,
        [((NY, 2 * COLS, COLS), BF16), ((NY, 2 * COLS, COLS), BF16)],
        [((COLS, ROWS), BF16)],
        2 * ROWS * 4096 * COLS,
        [VMEM] * 12,
    )
    gw_back = shift(gw_give, "core", 1)

    gw0, gw1, gw2, gw3 = call(
        chip_sum_kernel, "chip_sum", [gw_keep, gw_back], [((2 * COLS, COLS), F32)] + [((2 * COLS, COLS), BF16)] * 3
    )
    gw_rows = [shift(gw1, "y", 1), shift(gw2, "y", 2), shift(gw3, "y", 3)]

    block = ((PAIR, 2 * HD), BF16)
    scratch = [prob_kind, prob_kind]
    flops = NQ * PAIR
    gq, grad_out, row_dot, part3 = call(
        backward_far_kernel,
        "backward_far",
        [q_own, q_far] + dos + [lse, att, m3, kvs[3], prob3],
        [acc_kind, ((NQ, HD), BF16), row_kind, block],
        scratch,
        flops,
        vmem=16,
        after=[gw1],
    )
    back3 = shift(part3, "y", 2)
    gq, part1, part2 = call(
        backward_near_kernel,
        "backward_near",
        [q_own, q_far, grad_out, row_dot, lse, m1, kvs[1], kvs[2], prob1, prob2, gq],
        [acc_kind, block, block],
        scratch,
        2 * flops,
        vmem=16,
    )
    backs = [shift(part1, "y", -1), shift(part2, "y", 1), back3]
    gw_pair, gw_send = call(
        row_pair_kernel, "row_pair", [gw0] + gw_rows, [((COLS, COLS), F32), ((COLS, COLS), BF16)]
    )
    gw_far = shift(gw_send, "x_lo", 1)
    gq_keep, gq_give, part0 = call(
        backward_own_kernel,
        "backward_own",
        [q_own, q_far, grad_out, row_dot, lse, m0, kvs[0], prob0, gq],
        [((PAIR, HD), F32), ((PAIR, HD), BF16), ((PAIR, 2 * HD), F32)],
        [acc_kind] + scratch,
        flops,
        vmem=16,
        after=[gw_pair, back3, gw_far, gw_rows[1]],
    )
    gq_back = shift(gq_give, "x_lo", 1)
    (grad_out_weight,) = call(weight_sum_kernel, "weight_sum", [gw_pair, gw_far], [((COLS, COLS), F32)])
    keep, give = call(
        row_sum_kernel,
        "row_sum",
        [gq_keep, gq_back, part0] + backs,
        [((ROWS, 3 * HD), BF16), ((ROWS, 3 * HD), BF16)],
        after=[grad_out_weight],
    )
    grad_queries, grad_keys, grad_values = call(
        finish_kernel, "finish", [keep, shift(give, "core", 1)], [((ROWS, COLS), BF16)] * 3
    )
    return grad_queries, grad_keys, grad_values, grad_out_weight


def solution(mesh):
    devices = mesh.devices.reshape(NY, 2, 2, 2, NZ)
    fine = Mesh(devices, ("y", "x_lo", "core", "x_hi", "z"))
    ctx, head = ("y", "x_lo", "core"), ("x_hi", "z")
    return jax.shard_map(
        on_device,
        mesh=fine,
        in_specs=(
            P(ctx, head),
            P(ctx, head),
            P(ctx, head),
            P(ctx, head),
            P(head, None),
            P(),
            P(ctx),
        ),
        out_specs=(P(ctx, head), P(ctx, head), P(ctx, head), P(head, ctx)),
        check_vma=False,
    )
```

```python
import functools
import math

import jax
import jax.numpy as jnp
from jax import lax
from jax.experimental import pallas as pl
from jax.experimental.pallas import tpu as pltpu
from jax.sharding import Mesh, PartitionSpec as P

ROWS = 320
PAIR = 640
HD = 128
NQ = 1280
COLS = 256
FACTOR = HD ** -0.5
SCALE2 = FACTOR * math.log2(math.e)
FLOOR = -1e30
BIG = 1e37
NY = 4
NZ = 8

F32 = jnp.float32
BF16 = jnp.bfloat16

NT = (((1,), (1,)), ((), ()))
NN = (((1,), (0,)), ((), ()))
TN = (((0,), (0,)), ((), ()))


def dot(a, b, dims):
    return lax.dot_general(a, b, dims, preferred_element_type=F32)


BLOCK_Y = (0, NY - 1, 1, 2)


def token_of(base, row):
    turned = row + lax.axis_index("core") * ROWS
    return base + jnp.where(turned >= PAIR, turned - PAIR, turned)


def key_base(block):
    return lax.rem(lax.axis_index("y") + BLOCK_Y[block], NY) * NQ + lax.axis_index("x_lo") * PAIR


def own_docs(base, lengths):
    column = lax.broadcasted_iota(jnp.int32, (1, HD), 1)
    first, last = jnp.zeros((1, HD), jnp.int32), jnp.zeros((1, HD), jnp.int32)
    start = 0
    for i in range(8):
        first = jnp.where(column == i, start, first)
        start = start + lengths[i]
        last = jnp.where(column == i, start, last)
    token = token_of(base, lax.broadcasted_iota(jnp.int32, (PAIR, HD), 0))
    return (token >= first) & (token < last), column < 8


def fill_keys(wide, kv_ref, block, lengths):
    own, _ = own_docs(key_base(block), lengths)
    wide[:, :HD] = kv_ref[:, :HD]
    wide[:, HD:] = jnp.where(own, 1.0, 0.0).astype(BF16)


def fill_queries(wide, queries, lengths):
    for half, (here, q_ref) in enumerate(zip(HALVES, queries)):
        base = lax.axis_index("y") * NQ + jnp.where(lax.axis_index("x_lo") == half, 0, PAIR)
        own, listed = own_docs(base, lengths)
        wide[here, :HD] = q_ref[...]
        wide[here, HD:] = jnp.where(own, 0.0, jnp.where(listed, -BIG, 0.0)).astype(BF16)


def columns_of(core):
    return pl.ds(pl.multiple_of(core * HD, HD), HD)


HALVES = (slice(0, PAIR), slice(PAIR, NQ))


def join_kernel(held_ref, back_ref, kv_ref, own_ref):
    for rows, ref in ((slice(0, ROWS), held_ref), (slice(ROWS, PAIR), back_ref)):
        kv_ref[rows, :] = ref[:, : 2 * HD]
        own_ref[rows, :] = ref[:, 2 * HD :]


def stack_kernel(parts, *refs):
    out_ref, first = refs[-1], 0
    for ref, (start, count) in zip(refs[:-1], parts):
        out_ref[first : first + count, :] = ref[start : start + count, :]
        first += count


def forward_step(blocks, lengths, wide_q, wide_k, kvs, before, after, probs):
    for block, kv_ref, wide in zip(blocks, kvs, wide_k):
        fill_keys(wide, kv_ref, block, lengths)
    acc_in, m_in, l_in = before
    acc, m_ref, l_ref = after
    turned = [kv_ref[:, HD:].T for kv_ref in kvs]
    for here in (slice(0, 256), slice(256, 512), slice(512, 768), slice(768, 1024), slice(1024, NQ)):
        scores = [dot(wide[...], wide_q[here, :], NT) * SCALE2 for wide in wide_k]
        new = m_in[:, here]
        for s in scores:
            new = jnp.maximum(new, jnp.max(s, axis=0, keepdims=True))
        shrink = jnp.exp2(m_in[:, here] - new)
        total, out = l_in[:, here] * shrink, acc_in[:, here] * shrink
        for s, vals, prob_ref in zip(scores, turned, probs):
            p = jnp.exp2(s - new)
            total = total + jnp.sum(p, axis=0, keepdims=True)
            kept = p.astype(BF16)
            prob_ref[:, here] = kept
            out = out + dot(vals, kept, NN)
        m_ref[:, here], l_ref[:, here], acc[:, here] = new, total, out


def forward_own_kernel(lengths, q_own, q_far, kv, wide_q, acc, m_ref, l_ref, prob, wide_k, acc0, m0, l0):
    fill_queries(wide_q, (q_own, q_far), lengths)
    acc0[...] = jnp.zeros_like(acc0)
    m0[...] = jnp.full_like(m0, FLOOR)
    l0[...] = jnp.zeros_like(l0)
    forward_step((0,), lengths, wide_q, (wide_k,), (kv,), (acc0, m0, l0), (acc, m_ref, l_ref), (prob,))


def forward_near_kernel(lengths, wide_q, kv1, kv2, acc0, m0, l0, acc, m_ref, l_ref, prob1, prob2, wide1, wide2):
    forward_step((1, 2), lengths, wide_q, (wide1, wide2), (kv1, kv2), (acc0, m0, l0), (acc, m_ref, l_ref), (prob1, prob2))


def forward_far_kernel(lengths, wide_q, kv, acc0, m0, l0, out_ref, m_ref, prob, wide_k, acc, l_ref):
    forward_step((3,), lengths, wide_q, (wide_k,), (kv,), (acc0, m0, l0), (acc, m_ref, l_ref), (prob,))
    total = l_ref[...]
    seen = total > 0
    safe = jnp.where(seen, total, 1.0)
    out_ref[:HD, :] = (acc[...] * (1.0 / safe)).astype(BF16)
    rest = jnp.where(seen, m_ref[...] + jnp.log2(safe), FLOOR)
    parts = []
    for _ in range(3):
        part = rest.astype(BF16).astype(F32)
        parts.append(part)
        rest = rest - part
    parts.append(jnp.zeros((13, NQ), F32))
    out_ref[HD:, :] = jnp.concatenate(parts, axis=0).astype(BF16)


def merge_kernel(mine, theirs, att_ref, lse_ref, keep_ref, give_ref):
    def log_total(ref, columns):
        parts = ref[HD:, columns].astype(F32)
        return parts[0:1] + parts[1:2] + parts[2:3]

    for half in range(2):
        here, there = HALVES[half], HALVES[1 - half]
        a, b = log_total(mine, here), log_total(theirs, there)
        top = jnp.maximum(a, b)
        lse = top + jnp.log2(jnp.exp2(a - top) + jnp.exp2(b - top))
        lse_ref[:, here] = lse
        att = mine[:HD, here].astype(F32) * jnp.exp2(a - lse) + theirs[:HD, there].astype(F32) * jnp.exp2(b - lse)
        att = att.astype(BF16)
        att_ref[:, here] = att
        if half == 0:
            keep_ref[...] = att[:, :ROWS]
            give_ref[...] = att[:, ROWS:]


NEAR = ((0, 0, 0), (1, 0, ROWS), (-1, 0, 2 * ROWS), (2, 1, 0), (-2, 1, ROWS), (3, 2, 0), (-3, 3, 0), (4, 4, 0))
FAR = ((0, 5, 0), (1, 5, ROWS), (-1, 5, 2 * ROWS), (2, 6, 0), (-2, 6, ROWS), (3, 7, ROWS // 2), (-3, 8, ROWS // 2), (4, 9, 0))


def pieces_of(refs):
    own = lax.axis_index("x_hi")
    for x_hi, listed in ((own, NEAR), (1 - own, FAR)):
        for distance, i, first in listed:
            z = lax.rem(lax.axis_index("z") - distance + NZ, NZ)
            yield x_hi, z, distance % 2, refs[i][first : first + ROWS, :]


def dout_kernel(w, *refs):
    pieces, (keep_ref, give_ref, acc) = refs[:10], refs[10:]
    total = jnp.zeros((ROWS, COLS), F32)
    for x_hi, z, _, piece in pieces_of(pieces):
        columns = pl.ds(pl.multiple_of((x_hi * NZ + z) * COLS, COLS), COLS)
        total = total + dot(piece, w[:, columns], NT)
    acc[...] = total
    core = lax.axis_index("core")
    keep_ref[...] = acc[:, columns_of(core)].astype(BF16)
    give_ref[...] = acc[:, columns_of(1 - core)].astype(BF16)


def weight_kernel(att_own, att_other, *refs):
    pieces, (keep_ref, give_ref, both) = refs[:10], refs[10:]
    core = lax.axis_index("core")
    both[columns_of(core), :] = att_own[...]
    both[columns_of(1 - core), :] = att_other[...]
    y, x_lo = lax.axis_index("y"), lax.axis_index("x_lo")

    def run(same, other):
        for x_hi, z, odd, piece in pieces_of(pieces):
            first = jnp.where(lax.rem(z // 2, 2) == x_lo, 0, COLS)
            rows = pl.ds(pl.multiple_of(first, COLS), COLS)
            (other if odd else same)[lax.rem(x_hi * 2 + z // 4 - y + NY, NY), rows, :] = dot(both[...], piece, NN).astype(BF16)

    alike = lax.rem(lax.axis_index("z"), 2) == core
    pl.when(alike)(lambda: run(keep_ref, give_ref))
    pl.when(jnp.logical_not(alike))(lambda: run(give_ref, keep_ref))


def chip_sum_kernel(keep, back, own_ref, *send_refs):
    own_ref[...] = keep[0].astype(F32) + back[0].astype(F32)
    for i, ref in enumerate(send_refs):
        ref[...] = (keep[i + 1].astype(F32) + back[i + 1].astype(F32)).astype(BF16)


def row_pair_kernel(own, back1, back2, back3, own_ref, send_ref):
    for rows, ref in ((slice(0, COLS), own_ref), (slice(COLS, 2 * COLS), send_ref)):
        total = own[rows, :]
        for back in (back1, back2, back3):
            total = total + back[rows, :].astype(F32)
        ref[...] = total.astype(ref.dtype)


def backward_step(queries, grad_out, row_dot, lse_ref, gq_ref, m_ref, kvs, probs, gkv_refs, scratch):
    prob, score = scratch
    scale = jnp.exp2(m_ref[...] - lse_ref[...])
    for kv_ref, kept, gkv_ref in zip(kvs, probs, gkv_refs):
        keys, vals = kv_ref[:, :HD], kv_ref[:, HD:]
        gk = jnp.zeros((PAIR, HD), F32)
        for here, q_ref in zip(HALVES, queries):
            p = kept[:, here].astype(F32) * scale[:, here]
            prob[:, here] = p.astype(BF16)
            part = (p * (dot(vals, grad_out[here, :], NT) - row_dot[:, here])).astype(BF16)
            score[:, here] = part
            gk = gk + dot(part, q_ref[...], NN)
        gq_ref[...] += dot(keys, score[...], TN)
        gkv_ref[:, :HD] = (gk * FACTOR).astype(gkv_ref.dtype)
        gkv_ref[:, HD:] = dot(prob[...], grad_out[...], NN).astype(gkv_ref.dtype)


def backward_far_kernel(
    q_own, q_far, do0, do1, do2, do3, lse_ref, att_ref, m_ref, kv, kept, gq_ref, grad_out, row_dot, gkv_ref, *scratch
):
    for i, ref in enumerate((do0, do1, do2, do3)):
        grad_out[i * ROWS : (i + 1) * ROWS, :] = ref[...]
    for here in HALVES:
        turned = grad_out[here, :].astype(F32).T
        row_dot[:, here] = jnp.sum(turned * att_ref[:, here].astype(F32), axis=0, keepdims=True)
    gq_ref[...] = jnp.zeros_like(gq_ref)
    backward_step((q_own, q_far), grad_out, row_dot, lse_ref, gq_ref, m_ref, (kv,), (kept,), (gkv_ref,), scratch)


def backward_near_kernel(
    q_own, q_far, grad_out, row_dot, lse_ref, m_ref, kv1, kv2, kept1, kept2, gq_in, gq_ref, gkv1, gkv2, *scratch
):
    gq_ref[...] = gq_in[...]
    backward_step(
        (q_own, q_far), grad_out, row_dot, lse_ref, gq_ref, m_ref, (kv1, kv2), (kept1, kept2), (gkv1, gkv2), scratch
    )


def backward_own_kernel(
    q_own, q_far, grad_out, row_dot, lse_ref, m_ref, kv, kept, gq_in, gq_keep, gq_give, gkv_ref, gq_ref, *scratch
):
    gq_ref[...] = gq_in[...]
    backward_step((q_own, q_far), grad_out, row_dot, lse_ref, gq_ref, m_ref, (kv,), (kept,), (gkv_ref,), scratch)
    gq_keep[...] = (gq_ref[:, :PAIR] * FACTOR).T
    gq_give[...] = (gq_ref[:, PAIR:] * FACTOR).T.astype(BF16)


def row_sum_kernel(gq, gq_back, gkv, back1, back2, back3, keep_ref, give_ref):
    for rows, ref in ((slice(0, ROWS), keep_ref), (slice(ROWS, PAIR), give_ref)):
        ref[:, :HD] = (gq[rows, :] + gq_back[rows, :].astype(F32)).astype(BF16)
        total = gkv[rows, :]
        for back in (back1, back2, back3):
            total = total + back[rows, :].astype(F32)
        ref[:, HD:] = total.astype(BF16)


def finish_kernel(keep, back, gq_ref, gk_ref, gv_ref):
    core = lax.axis_index("core")
    here, there = columns_of(core), columns_of(1 - core)
    for i, ref in enumerate((gq_ref, gk_ref, gv_ref)):
        ref[:, here] = keep[:, i * HD : (i + 1) * HD]
        ref[:, there] = back[:, i * HD : (i + 1) * HD]


def weight_sum_kernel(own, back, out_ref):
    out_ref[...] = own[...] + back[...].astype(F32)


SMEM = pl.BlockSpec(memory_space=pltpu.SMEM)
VMEM = pl.BlockSpec(memory_space=pltpu.VMEM)
ANY = pl.BlockSpec(memory_space=pl.ANY)


def call(kernel, name, arrays, outs, scratch=(), flops=1e6, specs=None, vmem=12, after=()):
    moved = sum(a.size * a.dtype.itemsize for a in arrays) + sum(math.prod(s) * jnp.dtype(t).itemsize for s, t in outs)
    count, arrays, specs = len(arrays), list(arrays), specs or [VMEM] * len(arrays)

    def body(*refs):
        kernel(*refs[:count], *refs[count + len(after) :])

    return pl.pallas_call(
        body,
        name=name,
        out_shape=[jax.ShapeDtypeStruct(s, t) for s, t in outs],
        in_specs=specs + [ANY] * len(after),
        out_specs=[VMEM] * len(outs),
        scratch_shapes=[pltpu.VMEM(*item) if isinstance(item, tuple) else item for item in scratch],
        cost_estimate=pl.CostEstimate(flops=int(flops), bytes_accessed=int(moved), transcendentals=0),
        compiler_params=pltpu.CompilerParams(vmem_limit_bytes=vmem * 1024 * 1024),
    )(*arrays, *after)


def shift(x, axis, step):
    size = {"y": NY, "x_lo": 2, "core": 2, "x_hi": 2, "z": NZ}[axis]
    return lax.ppermute(x, axis, [(i, (i + step) % size) for i in range(size)])


def swap_both(x):
    return lax.ppermute(x, ("x_lo", "core"), [(i, 3 - i) for i in range(4)])


def stack(*parts, after=()):
    parts = [part if isinstance(part, tuple) else (part, 0, part.shape[0]) for part in parts]
    ranges = [(first, count) for _, first, count in parts]
    rows = sum(count for _, count in ranges)
    return call(functools.partial(stack_kernel, ranges), "stack", [p[0] for p in parts], [((rows, COLS), BF16)], after=after)[0]


def on_device(queries, keys, values, out_grad, out_weight, doc_lengths, loss_numer):
    scaled = (out_grad.astype(F32) * (loss_numer.astype(F32) / 8.0)[:, None]).astype(BF16)

    core = lax.axis_index("core")
    held, sent = (
        jnp.concatenate([lax.dynamic_slice_in_dim(a, which * HD, HD, 1) for a in (keys, values, queries)], axis=1)
        for which in (core, 1 - core)
    )
    kv, q_own = call(join_kernel, "join", [held, shift(sent, "core", 1)], [((PAIR, 2 * HD), BF16), ((PAIR, HD), BF16)])
    kvs = [kv, shift(kv, "y", 1), shift(kv, "y", -1), shift(kv, "y", 2)]
    q_far = shift(q_own, "x_lo", 1)

    up, down = [scaled], [scaled]
    for _ in range(3):
        up.append(shift(up[-1], "z", 1))
        down.append(shift(down[-1], "z", -1))
    half = ROWS // 2
    near = [stack(scaled, up[1], down[1], after=[]), stack(up[2], down[2], after=[kvs[3]])]
    far = [shift(a, "x_hi", 1) for a in near]
    up_last = shift(stack((up[3], 0, half), (far[1], 0, ROWS)), "z", 1)
    down_last = shift(stack((down[3], half, half), (far[1], ROWS, ROWS)), "z", -1)
    last = stack((up_last, 0, half), (down_last, 0, half))
    pieces = near + [up[3], down[3], last] + far + [up_last, down_last, shift(last, "x_hi", 1)]

    wide_q_kind, wide_k_kind = ((NQ, 2 * HD), BF16), ((PAIR, 2 * HD), BF16)
    acc_kind, row_kind, prob_kind = ((HD, NQ), F32), ((1, NQ), F32), ((PAIR, NQ), BF16)
    flops = 2 * 2 * NQ * PAIR * HD * 2
    wide_q, acc, m0, total, prob0 = call(
        forward_own_kernel,
        "forward_own",
        [doc_lengths, q_own, q_far, kvs[0]],
        [wide_q_kind, acc_kind, row_kind, row_kind, prob_kind],
        [wide_k_kind, acc_kind, row_kind, row_kind],
        flops,
        [SMEM] + [VMEM] * 3,
        16,
        after=[],
    )
    acc, m1, total, prob1, prob2 = call(
        forward_near_kernel,
        "forward_near",
        [doc_lengths, wide_q, kvs[1], kvs[2], acc, m0, total],
        [acc_kind, row_kind, row_kind, prob_kind, prob_kind],
        [wide_k_kind, wide_k_kind],
        2 * flops,
        [SMEM] + [VMEM] * 6,
        24,
        after=[],
    )
    out_part, m3, prob3 = call(
        forward_far_kernel,
        "forward_far",
        [doc_lengths, wide_q, kvs[3], acc, m1, total],
        [((HD + 16, NQ), BF16), row_kind, prob_kind],
        [wide_k_kind, acc_kind, row_kind],
        flops,
        [SMEM] + [VMEM] * 5,
        16,
        after=[far[1]],
    )
    att, lse, att_keep, att_give = call(
        merge_kernel,
        "merge",
        [out_part, shift(out_part, "x_lo", 1)],
        [((HD, NQ), BF16), row_kind, ((HD, ROWS), BF16), ((HD, ROWS), BF16)],
        after=[],
    )
    att_other = shift(att_give, "core", 1)

    do_keep, do_give = call(
        dout_kernel,
        "dout",
        [out_weight] + pieces,
        [((ROWS, HD), BF16), ((ROWS, HD), BF16)],
        [((ROWS, COLS), F32)],
        2 * ROWS * 4096 * COLS,
    )
    dos = [do_keep, shift(do_give, "core", 1), shift(do_keep, "x_lo", 1), swap_both(do_give)]

    gw_keep, gw_give = call(
        weight_kernel,
        "weight",
        [att_keep, att_other] + pieces,
        [((NY, 2 * COLS, COLS), BF16), ((NY, 2 * COLS, COLS), BF16)],
        [((COLS, ROWS), BF16)],
        2 * ROWS * 4096 * COLS,
        [VMEM] * 12,
    )
    gw_back = shift(gw_give, "core", 1)

    gw0, gw1, gw2, gw3 = call(
        chip_sum_kernel, "chip_sum", [gw_keep, gw_back], [((2 * COLS, COLS), F32)] + [((2 * COLS, COLS), BF16)] * 3
    )
    gw_rows = [shift(gw1, "y", 1), shift(gw2, "y", 2), shift(gw3, "y", 3)]

    block = ((PAIR, 2 * HD), BF16)
    scratch = [prob_kind, prob_kind]
    flops = NQ * PAIR
    gq, grad_out, row_dot, part3 = call(
        backward_far_kernel,
        "backward_far",
        [q_own, q_far] + dos + [lse, att, m3, kvs[3], prob3],
        [acc_kind, ((NQ, HD), BF16), row_kind, block],
        scratch,
        flops,
        vmem=16,
        after=[gw1],
    )
    back3 = shift(part3, "y", 2)
    gq, part1, part2 = call(
        backward_near_kernel,
        "backward_near",
        [q_own, q_far, grad_out, row_dot, lse, m1, kvs[1], kvs[2], prob1, prob2, gq],
        [acc_kind, block, block],
        scratch,
        2 * flops,
        vmem=16,
    )
    backs = [shift(part1, "y", -1), shift(part2, "y", 1), back3]
    gw_pair, gw_send = call(
        row_pair_kernel, "row_pair", [gw0] + gw_rows, [((COLS, COLS), F32), ((COLS, COLS), BF16)]
    )
    gw_far = shift(gw_send, "x_lo", 1)
    gq_keep, gq_give, part0 = call(
        backward_own_kernel,
        "backward_own",
        [q_own, q_far, grad_out, row_dot, lse, m0, kvs[0], prob0, gq],
        [((PAIR, HD), F32), ((PAIR, HD), BF16), ((PAIR, 2 * HD), F32)],
        [acc_kind] + scratch,
        flops,
        vmem=16,
        after=[gw_pair, back3, gw_far, gw_rows[1]],
    )
    gq_back = shift(gq_give, "x_lo", 1)
    (grad_out_weight,) = call(weight_sum_kernel, "weight_sum", [gw_pair, gw_far], [((COLS, COLS), F32)])
    keep, give = call(
        row_sum_kernel,
        "row_sum",
        [gq_keep, gq_back, part0] + backs,
        [((ROWS, 3 * HD), BF16), ((ROWS, 3 * HD), BF16)],
        after=[grad_out_weight],
    )
    grad_queries, grad_keys, grad_values = call(
        finish_kernel, "finish", [keep, shift(give, "core", 1)], [((ROWS, COLS), BF16)] * 3
    )
    return grad_queries, grad_keys, grad_values, grad_out_weight


def solution(mesh):
    devices = mesh.devices.reshape(NY, 2, 2, 2, NZ)
    fine = Mesh(devices, ("y", "x_lo", "core", "x_hi", "z"))
    ctx, head = ("y", "x_lo", "core"), ("x_hi", "z")
    return jax.shard_map(
        on_device,
        mesh=fine,
        in_specs=(
            P(ctx, head),
            P(ctx, head),
            P(ctx, head),
            P(ctx, head),
            P(head, None),
            P(),
            P(ctx),
        ),
        out_specs=(P(ctx, head), P(ctx, head), P(ctx, head), P(head, ctx)),
        check_vma=False,
    )
```
